128 devices in a mesh: fsdp: 64 (over z, y_lo, x, core), tp: 2 (over y_hi).
Axes of the slice: x: 4, y: 4 (y_hi: 2, y_lo: 2; y = y_hi * 2 + y_lo), z: 4, core: 2. Of those that a mesh axis runs over, the one named last changes fastest.
Arguments:
- tokens: bfloat16 [8192, 4096], P('fsdp', 'tp'), may hold values from -6 to 6
- cotangent: bfloat16 [8192, 4096], P('fsdp', 'tp'), may hold values from -6 to 6
- routes: int32 [8192, 1], P('fsdp'), may hold values from 0 to 15; in each aligned block of 128 rows (0 to 127, 128 to 255, ...) at most 12 rows name the same one
- gates: float32 [8192, 1], P('fsdp'), may hold values from 0.02 to 0.25
- gate_proj: bfloat16 [64, 1024, 1536], P('fsdp', None, 'tp'), may hold values from -0.09375 to 0.09375
- up_proj: bfloat16 [64, 1024, 1536], P('fsdp', None, 'tp'), may hold values from -0.09375 to 0.09375
- down_proj: bfloat16 [64, 1536, 1024], P('fsdp', 'tp'), may hold values from -0.15625 to 0.15625
- gate_dir: bfloat16 [64, 1024, 1536], P('fsdp', None, 'tp'), may hold values from -0.09375 to 0.09375
- up_dir: bfloat16 [64, 1024, 1536], P('fsdp', None, 'tp'), may hold values from -0.09375 to 0.09375
- down_dir: bfloat16 [64, 1536, 1024], P('fsdp', 'tp'), may hold values from -0.15625 to 0.15625
Outputs:
- hvp_gate: float32 [64, 1024, 1536], P('fsdp', None, 'tp')
- hvp_up: float32 [64, 1024, 1536], P('fsdp', None, 'tp')
- hvp_down: float32 [64, 1536, 1024], P('fsdp', 'tp')
The draws below stay inside these ranges and needn't reach their ends.
Inputs may be any that keep to these rules, and one draw needn't show every extreme that they name: `routes`: among the tokens of one device no expert is named more than 12 times.
All inputs are finite; a program needn't handle non-finite values.
Results may differ from the reference program's by a relative error of at most 0.0041.
Values may be sent and summed in bfloat16 or wider, within the bound.
A program may use at most 128 MiB of HBM per device.

```python
import math
import jax
import jax.numpy as jnp
import numpy as np
from jax import lax

D = 4096
FF = 1536
TOK_DEV = 128
EXPERTS = 16
CAP = 12
TOKENS = 8192
N_FSDP = 64


def level_of(own_key, dims, pieces, low, largest):
    def one(dim, parts):
        heights = jax.random.uniform(jax.random.fold_in(jax.random.fold_in(own_key, 6), dim), (parts,), jnp.float32, low / len(pieces), largest / len(pieces))
        return jnp.repeat(jnp.exp(heights), dims[dim] // parts).reshape((-1,) + (1,) * (len(dims) - dim - 1))

    gain = one(*pieces[0])
    for cut in pieces[1:]:
        gain = gain * one(*cut)
    return gain


def assign_block(key, own, number, rows, amount, top, bound, skew):
    order = jax.random.permutation(key, amount)
    packed, ordinary = shares(amount, rows * top, bound, skew, True), shares(amount, rows * top, bound, skew, False)
    places = jnp.arange(amount)

    def named(tallies, rotation):
        used = int((tallies > 0).sum())
        fixed = max(1, used // 4)
        shifted = fixed + (places - fixed + rotation * (used - fixed)) % max(1, amount - fixed)
        return jnp.zeros((amount,), jnp.int32).at[order[jnp.where(places < fixed, places, shifted)]].set(jnp.asarray(tallies, jnp.int32))

    tallies = jnp.where(number % 4 == 0, named(packed, number // 4), named(ordinary, number - number // 4 - 1))
    mixed = jax.random.permutation(jax.random.fold_in(own, 3), amount)
    source_of, sink = mixed[0:amount // 2 * 2:2], mixed[1:amount // 2 * 2:2]
    room = jnp.minimum(tallies[source_of] - 1, bound - tallies[sink]) // 2
    room = jnp.where((source_of == order[0]) | (sink == order[0]) | (tallies[sink] == 0), 0, jnp.maximum(room, 0))
    shifted = jax.random.randint(jax.random.fold_in(own, 4), (amount // 2,), 0, 1 << 20) % (room + 1)
    tallies = tallies.at[source_of].add(-shifted).at[sink].add(shifted)
    members = jnp.searchsorted(jnp.cumsum(tallies), jnp.arange(rows * top), side="right").astype(jnp.int32)
    listing = members.reshape(top, rows).T
    listing = listing[jax.random.permutation(jax.random.fold_in(own, 1), rows)]
    rotation = jax.random.randint(jax.random.fold_in(own, 2), (rows, 1), 0, top)
    return jnp.take_along_axis(listing, (jnp.arange(top)[None, :] + rotation) % top, axis=1)


def shares(number_of, total, reach, skew, full):
    loads = [(1 << 20) // math.isqrt(rank ** skew) + 1 for rank in range(1, number_of + 1)]
    largest = reach if full else min(reach, max(-(-total // number_of), total * loads[0] // sum(loads)))
    least = 1 if total - largest >= number_of - 1 else 0
    holding, rest = [largest] + [least] * (number_of - 1), total - largest - least * (number_of - 1)
    while rest > 0:
        movable = [i for i in range(1, number_of) if holding[i] < largest] or [i for i in range(1, number_of) if holding[i] < reach]
        pool, budget = sum([loads[i] for i in movable]), rest
        for i in movable:
            addition = min(reach - holding[i], max(1, budget * loads[i] // pool), rest)
            holding[i] = holding[i] + addition
            rest = rest - addition
    return np.array(holding)


def gaussian(rng, dims, scale, reach, pieces=(), held_as=jnp.bfloat16):
    level = level_of(rng, dims, pieces, -0.22, 0.18) if pieces else 1.0
    entries = jax.random.normal(rng, dims, jnp.float32) * scale * level
    return jnp.minimum(jnp.maximum(entries, -reach), reach).astype(held_as)


def setup_inputs(seed: int = 0) -> dict:
    keys = jax.random.split(jax.random.key(seed), 11)
    tokens = gaussian(keys[0], (TOKENS, D), 1.0, 6.0, ((0, 64), (1, 2)))
    cotangent = gaussian(keys[1], (TOKENS, D), 1.0, 6.0, ((0, 64), (1, 2)))
    routes_keys = jax.random.split(jax.random.fold_in(keys[2], 1), TOKENS // TOK_DEV)
    routes_turns = jax.random.permutation(jax.random.fold_in(keys[2], 3), TOKENS // TOK_DEV)
    routes = jax.vmap(lambda own, number: assign_block(jax.random.fold_in(keys[2], 2), own, number, TOK_DEV, EXPERTS, 1, CAP, 2))(routes_keys, routes_turns).reshape((TOKENS, 1))
    gates = jnp.clip(jnp.exp(math.log(0.25) - 2.5257287 * jax.random.uniform(keys[3], (TOKENS, 1), jnp.float32) ** level_of(keys[3], (TOKENS, 1), ((0, 64),), -0.2, 0.2)), 0.02, 0.25)
    gate_proj = gaussian(keys[4], (N_FSDP, D // 4, FF), D ** -0.5, 0.09375, ((0, 64), (2, 2)))
    up_proj = gaussian(keys[5], (N_FSDP, D // 4, FF), D ** -0.5, 0.09375, ((0, 64), (2, 2)))
    down_proj = gaussian(keys[6], (N_FSDP, FF, D // 4), FF ** -0.5, 0.15625, ((0, 64), (1, 2)))
    gate_dir = gaussian(keys[7], (N_FSDP, D // 4, FF), D ** -0.5, 0.09375, ((0, 64), (2, 2)))
    up_dir = gaussian(keys[8], (N_FSDP, D // 4, FF), D ** -0.5, 0.09375, ((0, 64), (2, 2)))
    down_dir = gaussian(keys[9], (N_FSDP, FF, D // 4), FF ** -0.5, 0.15625, ((0, 64), (1, 2)))
    return dict(tokens=tokens, cotangent=cotangent, routes=routes, gates=gates, gate_proj=gate_proj, up_proj=up_proj, down_proj=down_proj, gate_dir=gate_dir, up_dir=up_dir, down_dir=down_dir)


def curvature(stacked, hidden_width):
    gate_pre = stacked[:, 0:hidden_width]
    up_pre = stacked[:, hidden_width:2 * hidden_width]
    gate_tan = stacked[:, 2 * hidden_width:3 * hidden_width]
    up_tan = stacked[:, 3 * hidden_width:4 * hidden_width]
    grad_hidden = stacked[:, 4 * hidden_width:5 * hidden_width]
    tan_grad = stacked[:, 5 * hidden_width:6 * hidden_width]
    sigmoid_gate = jax.nn.sigmoid(gate_pre)
    silu_gate = gate_pre * sigmoid_gate
    slope = sigmoid_gate * (1.0 + gate_pre * (1.0 - sigmoid_gate))
    bend = sigmoid_gate * (1.0 - sigmoid_gate) * (2.0 + gate_pre * (1.0 - 2.0 * sigmoid_gate))
    tan_gate = tan_grad * up_pre * slope + grad_hidden * up_tan * slope + grad_hidden * up_pre * bend * gate_tan
    tan_up = tan_grad * silu_gate + grad_hidden * slope * gate_tan
    tan_hidden = slope * gate_tan * up_pre + silu_gate * up_tan
    return jnp.concatenate([tan_gate, tan_up, tan_hidden], axis=1).astype(jnp.bfloat16)


def reference(tokens, cotangent, routes, gates, gate_proj, up_proj, down_proj, gate_dir, up_dir, down_dir):
    row_limit = N_FSDP * CAP
    zero_row = jnp.zeros((1, D), jnp.bfloat16)
    tok_pad = jnp.concatenate([tokens, zero_row], axis=0)
    cot_pad = jnp.concatenate([cotangent, zero_row], axis=0)
    contract = (((0,), (0,)), ((), ()))
    against = (((1,), (1,)), ((), ()))

    def rows_of(stack, start):
        return lax.dynamic_slice_in_dim(stack, start, 4, 0).reshape(D, FF)

    def cols_of(stack, start):
        return lax.dynamic_slice_in_dim(stack, start, 4, 0).transpose(1, 0, 2).reshape(FF, D)

    def per_expert(expert):
        hit = routes == expert
        row_weight = jnp.sum(jnp.where(hit, gates, jnp.zeros_like(gates)), axis=1)
        chosen = jnp.any(hit, axis=1)
        row_index = jnp.nonzero(chosen, size=row_limit, fill_value=TOKENS)[0].astype(jnp.int32)
        rows_tok = tok_pad[row_index]
        weight_pad = jnp.concatenate([row_weight, jnp.zeros((1,), row_weight.dtype)])
        rows_cot = (weight_pad[row_index][:, None] * cot_pad[row_index].astype(jnp.float32)).astype(jnp.bfloat16)
        start = (expert * 4).astype(jnp.int32)
        forward_weights = jnp.concatenate([rows_of(gate_proj, start), rows_of(up_proj, start), rows_of(gate_dir, start), rows_of(up_dir, start)], axis=1)
        backward_weights = jnp.concatenate([cols_of(down_proj, start), cols_of(down_dir, start)], axis=0)
        stacked = jnp.concatenate([
            jnp.dot(rows_tok, forward_weights, preferred_element_type=jnp.float32),
            lax.dot_general(rows_cot, backward_weights, against, preferred_element_type=jnp.float32)], axis=1)
        curved = curvature(stacked, FF)
        hess_gate = lax.dot_general(rows_tok, curved[:, 0:FF], contract, preferred_element_type=jnp.float32)
        hess_up = lax.dot_general(rows_tok, curved[:, FF:2 * FF], contract, preferred_element_type=jnp.float32)
        hess_down = lax.dot_general(curved[:, 2 * FF:3 * FF], rows_cot, contract, preferred_element_type=jnp.float32)
        return (hess_gate.reshape(4, D // 4, FF), hess_up.reshape(4, D // 4, FF),
                hess_down.reshape(FF, 4, D // 4).transpose(1, 0, 2))

    hess_gate, hess_up, hess_down = lax.map(per_expert, jnp.arange(EXPERTS, dtype=jnp.int32))
    return (hess_gate.reshape(N_FSDP, D // 4, FF), hess_up.reshape(N_FSDP, D // 4, FF),
            hess_down.reshape(N_FSDP, FF, D // 4))
```

```python
import jax
import jax.numpy as jnp
from jax import lax
from jax.experimental import pallas as pl
from jax.experimental.pallas import tpu as pltpu
from jax.sharding import PartitionSpec as P

MESH = pl.DeviceIdType.MESH
CAPACITY = 12
BLOCK = 4 * CAPACITY
VMEM_LIMIT = 60 * 1024 * 1024
SPACE = pl.BlockSpec(memory_space=pltpu.VMEM)
HBM = pl.BlockSpec(memory_space=pl.ANY)


def dispatch_kernel(
    tok_ref, cot_ref, row_ref, col_ref, gate_ref, out_ref, send_ref, pick_ref, feed_ref, send_sem, recv_sem
):
    tokens, width = tok_ref.shape
    fine = width // 4
    groups = out_ref.shape[0] // BLOCK
    experts = groups // 4
    me, half = lax.axis_index("fsdp"), lax.axis_index("tp")
    source_half = (me % 4) // 2
    keeps_own = source_half == half

    barrier = pltpu.get_barrier_semaphore()

    def greet(other, carry):
        @pl.when(jnp.logical_or(other != me, source_half != half))
        def _():
            pl.semaphore_signal(barrier, inc=1, device_id=(other, source_half), device_id_type=MESH)

        return carry

    lax.fori_loop(0, groups, greet, 0)

    row, col = row_ref[...], col_ref[...]
    first = lax.broadcasted_iota(jnp.int32, (tokens, tokens), 0)
    second = lax.broadcasted_iota(jnp.int32, (tokens, tokens), 1)
    before = jnp.where((col == row) & (first < second), 1.0, 0.0)
    slot = row.astype(jnp.float32) * CAPACITY + jnp.sum(before, axis=0, keepdims=True)
    key = jnp.concatenate([slot + 1024.0 * part for part in range(4)], axis=1)
    place = lax.broadcasted_iota(jnp.int32, (experts * BLOCK, 1), 0).astype(jnp.float32)
    expert = jnp.floor((place + 0.5) * (1.0 / BLOCK))
    within = place - expert * BLOCK
    part = jnp.floor((within + 0.5) * (1.0 / CAPACITY))
    wanted = expert * CAPACITY + (within - part * CAPACITY) + 1024.0 * part
    pick_ref[...] = jnp.where(wanted == key, 1.0, 0.0).astype(jnp.bfloat16)
    weighted = (gate_ref[...] * cot_ref[...].astype(jnp.float32)).astype(jnp.bfloat16)
    for piece in range(2):
        for side in range(2):
            lanes = slice((2 * piece + side) * fine, (2 * piece + side + 1) * fine)
            feed_ref[piece, pl.ds(side * tokens, tokens), :] = tok_ref[:, lanes]
            feed_ref[piece, pl.ds((2 + side) * tokens, tokens), :] = weighted[:, lanes]

    pl.semaphore_wait(barrier, groups - jnp.where(keeps_own, 1, 0))

    def remote(expert, piece, side, number):
        target = 4 * expert + 2 * half + piece
        return pltpu.make_async_remote_copy(
            src_ref=send_ref.at[piece, pl.ds(pl.multiple_of(expert * BLOCK, BLOCK), BLOCK), :],
            dst_ref=out_ref.at[pl.ds(pl.multiple_of(me * BLOCK, BLOCK), BLOCK), :],
            send_sem=send_sem.at[number],
            recv_sem=recv_sem.at[me],
            device_id=(target, side),
            device_id_type=MESH,
        )

    def numbered(step):
        expert = (me // 4 + step) % experts
        return expert

    def send(step, carry):
        expert = numbered(step)
        base = pl.multiple_of(expert * BLOCK, BLOCK)
        for piece in range(2):
            send_ref[piece, pl.ds(base, BLOCK), :] = jnp.dot(
                pick_ref[pl.ds(base, BLOCK), :], feed_ref[piece], preferred_element_type=jnp.float32
            ).astype(jnp.bfloat16)
            for side in range(2):
                target = 4 * expert + 2 * half + piece
                here = jnp.logical_and(target == me, half == side)
                number = step * 4 + piece * 2 + side

                @pl.when(jnp.logical_not(here))
                def _():
                    remote(expert, piece, side, number).start()

                @pl.when(here)
                def _():
                    pltpu.make_async_copy(
                        send_ref.at[piece, pl.ds(base, BLOCK), :],
                        out_ref.at[pl.ds(pl.multiple_of(me * BLOCK, BLOCK), BLOCK), :],
                        recv_sem.at[me],
                    ).start()

        return carry

    lax.fori_loop(0, experts, send, 0)

    def drain(source, carry):
        block = out_ref.at[pl.ds(pl.multiple_of(source * BLOCK, BLOCK), BLOCK), :]
        pltpu.make_async_copy(block, block, recv_sem.at[source]).wait()
        return carry

    lax.fori_loop(0, groups, drain, 0)

    def sent(step, carry):
        expert = numbered(step)
        for piece in range(2):
            for side in range(2):
                target = 4 * expert + 2 * half + piece

                @pl.when(jnp.logical_not(jnp.logical_and(target == me, half == side)))
                def _():
                    remote(expert, piece, side, step * 4 + piece * 2 + side).wait_send()

        return carry

    lax.fori_loop(0, experts, sent, 0)


def curvature(total, width):
    gate_pre, up_pre, gate_tan, up_tan, grad_hidden, tan_grad = (
        total[:, width * place : width * (place + 1)] for place in range(6)
    )
    sigmoid_gate = jax.nn.sigmoid(gate_pre)
    silu_gate = gate_pre * sigmoid_gate
    slope = sigmoid_gate * (1.0 + gate_pre * (1.0 - sigmoid_gate))
    bend = sigmoid_gate * (1.0 - sigmoid_gate) * (2.0 + gate_pre * (1.0 - 2.0 * sigmoid_gate))
    tan_gate = (
        tan_grad * up_pre * slope
        + grad_hidden * up_tan * slope
        + grad_hidden * up_pre * bend * gate_tan
    )
    tan_up = tan_grad * silu_gate + grad_hidden * slope * gate_tan
    tan_hidden = slope * gate_tan * up_pre + silu_gate * up_tan
    return jnp.concatenate([tan_gate, tan_up, tan_hidden], axis=1).astype(jnp.bfloat16)


def group_kernel(
    packed_ref, gate_ref, up_ref, gdir_ref, udir_ref, down_ref, ddir_ref,
    tok_ref, cot_ref, curved_ref,
    fwd_ref, bwd_ref, keep_ref, core_out, core_in, chip_keep, chip_out, chip_in,
    load_sem, core_send, core_recv, chip_send, chip_recv, back_send, back_recv, last_send, last_recv,
):
    rows, depth = tok_ref.shape
    chunks, _, wide = curved_ref.shape
    slim = wide // 3
    halved, quarter = rows // 2, rows // 4
    me, side = lax.axis_index("fsdp"), lax.axis_index("tp")
    core, chip = me % 2, (me % 4) // 2
    core_mate = (me + 1 - 2 * core, side)
    chip_mate = (me + 2 - 4 * chip, side)

    def loads(chunk):
        at = slice(chunk * slim, (chunk + 1) * slim)
        pieces = [
            (ref.at[:, at], fwd_ref.at[chunk, :, pl.ds(place * slim, slim)])
            for place, ref in enumerate((gate_ref, up_ref, gdir_ref, udir_ref))
        ] + [
            (ref.at[at, :], bwd_ref.at[chunk, pl.ds(place * slim, slim), :])
            for place, ref in enumerate((down_ref, ddir_ref))
        ]
        return [
            pltpu.make_async_copy(source, target, load_sem.at[chunk, place])
            for place, (source, target) in enumerate(pieces)
        ]

    barrier = pltpu.get_barrier_semaphore()
    for mate in (core_mate, chip_mate):
        pl.semaphore_signal(barrier, inc=1, device_id=mate, device_id_type=MESH)
    for chunk in range(chunks):
        for copy in loads(chunk):
            copy.start()

    sort_rows = 4 * BLOCK
    left = lax.broadcasted_iota(jnp.int32, (sort_rows, 1), 0).astype(jnp.float32)
    source = jnp.floor((left + 0.5) * (1.0 / BLOCK))
    part = jnp.floor((left - source * BLOCK + 0.5) * (1.0 / CAPACITY))
    rest = left - source * BLOCK - part * CAPACITY
    out_part, out_source, out_rest = source, part, rest
    wanted = out_source * BLOCK + out_part * CAPACITY + out_rest
    have = lax.broadcasted_iota(jnp.int32, (1, sort_rows), 1).astype(jnp.float32)
    sorter = jnp.where(wanted == have, 1.0, 0.0).astype(jnp.bfloat16)
    fine = depth // 2

    def sort(group, carry):
        block = packed_ref[pl.ds(pl.multiple_of(group * sort_rows, sort_rows), sort_rows), :]
        ordered = jnp.dot(sorter, block, preferred_element_type=jnp.float32).astype(jnp.bfloat16)
        to = pl.ds(pl.multiple_of(group * BLOCK, BLOCK), BLOCK)
        tok_ref[to, 0:fine] = ordered[0:BLOCK]
        tok_ref[to, fine:depth] = ordered[BLOCK : 2 * BLOCK]
        cot_ref[to, 0:fine] = ordered[2 * BLOCK : 3 * BLOCK]
        cot_ref[to, fine:depth] = ordered[3 * BLOCK : 4 * BLOCK]
        return carry

    lax.fori_loop(0, rows // BLOCK, sort, 0)
    pl.semaphore_wait(barrier, 2)

    against = (((1,), (1,)), ((), ()))

    def to_core(chunk):
        return pltpu.make_async_remote_copy(
            src_ref=core_out.at[chunk], dst_ref=core_in.at[chunk],
            send_sem=core_send.at[chunk], recv_sem=core_recv.at[chunk],
            device_id=core_mate, device_id_type=MESH,
        )

    def to_chip(chunk):
        return pltpu.make_async_remote_copy(
            src_ref=chip_out.at[chunk], dst_ref=chip_in.at[chunk],
            send_sem=chip_send.at[chunk], recv_sem=chip_recv.at[chunk],
            device_id=chip_mate, device_id_type=MESH,
        )

    def back(chunk, where):
        place = curved_ref.at[chunk, pl.ds(pl.multiple_of(where, quarter), quarter), :]
        return pltpu.make_async_remote_copy(
            src_ref=place, dst_ref=place,
            send_sem=back_send.at[chunk], recv_sem=back_recv.at[chunk],
            device_id=chip_mate, device_id_type=MESH,
        )

    def last(chunk, where):
        place = curved_ref.at[chunk, pl.ds(pl.multiple_of(where, halved), halved), :]
        return pltpu.make_async_remote_copy(
            src_ref=place, dst_ref=place,
            send_sem=last_send.at[chunk], recv_sem=last_recv.at[chunk],
            device_id=core_mate, device_id_type=MESH,
        )

    my_half, mate_half = core * halved, (1 - core) * halved
    my_quarter = my_half + chip * quarter
    mate_quarter = my_half + (1 - chip) * quarter

    def forward(chunk, begin, into):
        at = pl.ds(pl.multiple_of(begin, halved), halved)
        into[chunk, :, 0 : 4 * slim] = jnp.dot(
            tok_ref[at, :], fwd_ref[chunk], preferred_element_type=jnp.float32
        )
        into[chunk, :, 4 * slim : 6 * slim] = lax.dot_general(
            cot_ref[at, :], bwd_ref[chunk], against, preferred_element_type=jnp.float32
        )

    def products(chunk):
        for place in range(6):
            pltpu.make_async_copy(
                bwd_ref.at[chunk, pl.ds(0, slim), :] if place >= 4 else fwd_ref.at[chunk, :, pl.ds(0, slim)],
                bwd_ref.at[chunk, pl.ds(0, slim), :] if place >= 4 else fwd_ref.at[chunk, :, pl.ds(0, slim)],
                load_sem.at[chunk, place],
            ).wait()
        forward(chunk, mate_half, core_out)
        to_core(chunk).start()
        forward(chunk, my_half, keep_ref)

    def core_sum(chunk):
        to_core(chunk).wait_recv()
        theirs = pl.ds(pl.multiple_of((1 - chip) * quarter, quarter), quarter)
        chip_out[chunk] = (keep_ref[chunk, theirs, :] + core_in[chunk, theirs, :]).astype(jnp.bfloat16)
        to_chip(chunk).start()
        ours = pl.ds(pl.multiple_of(chip * quarter, quarter), quarter)
        chip_keep[chunk] = keep_ref[chunk, ours, :] + core_in[chunk, ours, :]

    def first_pass(step, carry):
        @pl.when(step < chunks)
        def _():
            products(step)

        @pl.when(step > 0)
        def _():
            core_sum(step - 1)

        return carry

    lax.fori_loop(0, chunks + 1, first_pass, 0)

    def curve(chunk, carry):
        to_chip(chunk).wait_recv()
        total = chip_keep[chunk] + chip_in[chunk].astype(jnp.float32)
        curved_ref[chunk, pl.ds(pl.multiple_of(my_quarter, quarter), quarter), :] = curvature(total, slim)
        back(chunk, my_quarter).start()
        return carry

    lax.fori_loop(0, chunks, curve, 0)

    def spread(chunk, carry):
        back(chunk, mate_quarter).wait_recv()
        last(chunk, my_half).start()
        return carry

    lax.fori_loop(0, chunks, spread, 0)

    def finish(chunk, carry):
        last(chunk, mate_half).wait_recv()
        to_core(chunk).wait_send()
        to_chip(chunk).wait_send()
        back(chunk, my_quarter).wait_send()
        last(chunk, my_half).wait_send()
        return carry

    lax.fori_loop(0, chunks, finish, 0)


def product_kernel(tok_ref, cot_ref, curved_ref, gate_out, up_out, down_out, flipped):
    slim = curved_ref.shape[2] // 3

    @pl.when(pl.program_id(0) == 0)
    def _():
        flipped[...] = tok_ref[...].T

    both = jnp.dot(flipped[...], curved_ref[0, :, 0 : 2 * slim], preferred_element_type=jnp.float32)
    gate_out[...] = both[:, 0:slim]
    up_out[...] = both[:, slim : 2 * slim]
    down_out[...] = lax.dot_general(
        curved_ref[0, :, 2 * slim : 3 * slim],
        cot_ref[...],
        (((0,), (0,)), ((), ())),
        preferred_element_type=jnp.float32,
    )


def local(
    tokens, cotangent, routes, gates, gate_proj, up_proj, down_proj, gate_dir, up_dir, down_dir
):
    count, width = tokens.shape
    groups = lax.axis_size("fsdp")
    experts = groups // 4
    depth, hidden = gate_proj.shape[1:]
    rows = groups * CAPACITY
    slim = 128
    chunks = hidden // slim
    halved, quarter = rows // 2, rows // 4
    bf16, f32 = jnp.bfloat16, jnp.float32

    packed = pl.pallas_call(
        dispatch_kernel,
        name="dispatch",
        out_shape=jax.ShapeDtypeStruct((groups * BLOCK, width // 4), bf16),
        in_specs=[SPACE] * 5,
        out_specs=HBM,
        scratch_shapes=[
            pltpu.VMEM((2, experts * BLOCK, width // 4), bf16),
            pltpu.VMEM((experts * BLOCK, 4 * count), bf16),
            pltpu.VMEM((2, 4 * count, width // 4), bf16),
            pltpu.SemaphoreType.DMA((groups,)),
            pltpu.SemaphoreType.DMA((groups,)),
        ],
        compiler_params=pltpu.CompilerParams(
            collective_id=0, has_side_effects=True, vmem_limit_bytes=VMEM_LIMIT
        ),
    )(tokens, cotangent, routes.reshape(1, count), routes, gates)

    tok, cot, curved = pl.pallas_call(
        group_kernel,
        name="group",
        out_shape=(
            jax.ShapeDtypeStruct((rows, depth), bf16),
            jax.ShapeDtypeStruct((rows, depth), bf16),
            jax.ShapeDtypeStruct((chunks, rows, 3 * slim), bf16),
        ),
        in_specs=[SPACE] + [HBM] * 6,
        out_specs=(SPACE,) * 3,
        scratch_shapes=[
            pltpu.VMEM((chunks, depth, 4 * slim), bf16),
            pltpu.VMEM((chunks, 2 * slim, depth), bf16),
            pltpu.VMEM((chunks, halved, 6 * slim), f32),
            pltpu.VMEM((chunks, halved, 6 * slim), f32),
            pltpu.VMEM((chunks, halved, 6 * slim), f32),
            pltpu.VMEM((chunks, quarter, 6 * slim), f32),
            pltpu.VMEM((chunks, quarter, 6 * slim), bf16),
            pltpu.VMEM((chunks, quarter, 6 * slim), bf16),
            pltpu.SemaphoreType.DMA((chunks, 6)),
        ]
        + [pltpu.SemaphoreType.DMA((chunks,))] * 8,
        compiler_params=pltpu.CompilerParams(
            collective_id=1, has_side_effects=True, vmem_limit_bytes=VMEM_LIMIT
        ),
    )(packed, gate_proj[0], up_proj[0], gate_dir[0], up_dir[0], down_proj[0], down_dir[0])

    whole = lambda chunk: (0, 0)
    hess_gate, hess_up, hess_down = pl.pallas_call(
        product_kernel,
        name="products",
        grid=(chunks,),
        out_shape=(
            jax.ShapeDtypeStruct((depth, hidden), f32),
            jax.ShapeDtypeStruct((depth, hidden), f32),
            jax.ShapeDtypeStruct((hidden, depth), f32),
        ),
        in_specs=[
            pl.BlockSpec((rows, depth), whole),
            pl.BlockSpec((rows, depth), whole),
            pl.BlockSpec((1, rows, 3 * slim), lambda chunk: (chunk, 0, 0)),
        ],
        out_specs=(
            pl.BlockSpec((depth, slim), lambda chunk: (0, chunk)),
            pl.BlockSpec((depth, slim), lambda chunk: (0, chunk)),
            pl.BlockSpec((slim, depth), lambda chunk: (chunk, 0)),
        ),
        scratch_shapes=[pltpu.VMEM((depth, rows), bf16)],
        compiler_params=pltpu.CompilerParams(vmem_limit_bytes=VMEM_LIMIT),
    )(tok, cot, curved)
    return (hess_gate[None], hess_up[None], hess_down[None])


def solution(mesh):
    return jax.shard_map(
        local,
        mesh=mesh,
        in_specs=(
            P("fsdp", "tp"),
            P("fsdp", "tp"),
            P("fsdp", None),
            P("fsdp", None),
            P("fsdp", None, "tp"),
            P("fsdp", None, "tp"),
            P("fsdp", "tp", None),
            P("fsdp", None, "tp"),
            P("fsdp", None, "tp"),
            P("fsdp", "tp", None),
        ),
        out_specs=(P("fsdp", None, "tp"), P("fsdp", None, "tp"), P("fsdp", "tp", None)),
        check_vma=False,
    )
```

```python
import jax
import jax.numpy as jnp
from jax import lax
from jax.experimental import pallas as pl
from jax.experimental.pallas import tpu as pltpu
from jax.sharding import PartitionSpec as P

MESH = pl.DeviceIdType.MESH
CAPACITY = 12
BLOCK = 4 * CAPACITY
VMEM_LIMIT = 60 * 1024 * 1024
SPACE = pl.BlockSpec(memory_space=pltpu.VMEM)
HBM = pl.BlockSpec(memory_space=pl.ANY)


def dispatch_kernel(
    tok_ref, cot_ref, route_ref, gate_ref, out_ref, send_ref, pick_ref, feed_ref, relay_ref,
    send_sem, recv_sem, pass_send, pass_recv,
):
    tokens, width = tok_ref.shape
    fine = width // 4
    groups = out_ref.shape[0] // BLOCK
    experts = groups // 4
    me, high = lax.axis_index("fsdp"), lax.axis_index("tp")
    z, low, x, core = me // 16, (me // 8) % 2, (me // 2) % 4, me % 2
    y = high * 2 + low

    def plane(to_z, to_y):
        return to_z * 16 + (to_y % 2) * 8 + x * 2 + core, to_y // 2

    def beside(to_x, to_core):
        return me - x * 2 - core + to_x * 2 + to_core, high

    barrier = pltpu.get_barrier_semaphore()
    for step in range(1, 16):
        pl.semaphore_signal(
            barrier, inc=1, device_id=plane((z + step // 4) % 4, (y + step % 4) % 4), device_id_type=MESH
        )
    for step in range(1, 8):
        pl.semaphore_signal(
            barrier, inc=1, device_id=beside((x + step // 2) % 4, (core + step) % 2), device_id_type=MESH
        )

    row = route_ref[...].astype(jnp.float32)
    col = jnp.broadcast_to(row, (tokens, tokens)).T
    first = lax.broadcasted_iota(jnp.int32, (tokens, tokens), 0)
    second = lax.broadcasted_iota(jnp.int32, (tokens, tokens), 1)
    before = jnp.where((col == row) & (first < second), 1.0, 0.0)
    slot = row * CAPACITY + jnp.sum(before, axis=0, keepdims=True)
    key = jnp.concatenate([slot + 1024.0 * part for part in range(4)], axis=1)
    place = lax.broadcasted_iota(jnp.int32, (experts * BLOCK, 1), 0).astype(jnp.float32)
    expert = jnp.floor((place + 0.5) * (1.0 / BLOCK))
    within = place - expert * BLOCK
    part = jnp.floor((within + 0.5) * (1.0 / CAPACITY))
    wanted = expert * CAPACITY + (within - part * CAPACITY) + 1024.0 * part
    pick_ref[...] = jnp.where(wanted == key, 1.0, 0.0).astype(jnp.bfloat16)
    gate = jnp.broadcast_to(gate_ref[...], (tokens, tokens)).T[:, 0:1]
    weighted = (gate * cot_ref[...].astype(jnp.float32)).astype(jnp.bfloat16)
    for piece in range(2):
        for side in range(2):
            lanes = slice((2 * piece + side) * fine, (2 * piece + side + 1) * fine)
            feed_ref[piece, pl.ds(side * tokens, tokens), :] = tok_ref[:, lanes]
            feed_ref[piece, pl.ds((2 + side) * tokens, tokens), :] = weighted[:, lanes]

    def gather(step, carry):
        at = pl.ds(pl.multiple_of(step * 4 * BLOCK, 4 * BLOCK), 4 * BLOCK)
        for piece in range(2):
            send_ref[piece, at, :] = jnp.dot(
                pick_ref[at, :], feed_ref[piece], preferred_element_type=jnp.float32
            ).astype(jnp.bfloat16)
        return carry

    lax.fori_loop(0, experts // 4, gather, 0)
    pl.semaphore_wait(barrier, 22)

    def block(number, count=1):
        return pl.ds(pl.multiple_of(number * BLOCK, BLOCK), count * BLOCK)

    def pair_of(stage):
        return (x // 2 + 1 + stage // 2) % 2, (core + stage) % 2

    def moves(number):
        stage, step = number // 16, number % 16
        return stage, step % 4, (step // 4 + step) % 4

    def outward(number):
        stage, dz, dy = moves(number)
        pair, to_core = pair_of(stage)
        to_z, to_y = (z + dz) % 4, (y + dy) % 4
        slot = stage * 16 + z * 4 + y
        source = send_ref.at[to_core, block(to_z * 4 + (to_y % 2) * 2 + pair), :]
        target = relay_ref.at[block(slot), :]
        here = jnp.logical_and(dz == 0, dy == 0)
        local_copy = lambda: pltpu.make_async_copy(source, target, recv_sem.at[slot])
        remote_copy = lambda: pltpu.make_async_remote_copy(
            src_ref=source, dst_ref=target, send_sem=send_sem.at[number], recv_sem=recv_sem.at[slot],
            device_id=plane(to_z, to_y), device_id_type=MESH,
        )
        return here, local_copy, remote_copy

    def along(number):
        stage, dz, dy = moves(number)
        pair, to_core = pair_of(stage)
        from_z, from_y = (z + 4 - dz) % 4, (y + 4 - dy) % 4
        slot = stage * 16 + from_z * 4 + from_y
        origin = from_z * 16 + (from_y % 2) * 8 + x * 2 + core
        to_x = pair * 2 + from_y // 2
        source, target = relay_ref.at[block(slot), :], out_ref.at[block(origin), :]
        here = jnp.logical_and(to_x == x, to_core == core)
        local_copy = lambda: pltpu.make_async_copy(source, target, pass_recv.at[origin])
        remote_copy = lambda: pltpu.make_async_remote_copy(
            src_ref=source, dst_ref=target, send_sem=pass_send.at[number], recv_sem=pass_recv.at[origin],
            device_id=beside(to_x, to_core), device_id_type=MESH,
        )
        return slot, here, local_copy, remote_copy

    def send(number, carry):
        here, local_copy, remote_copy = outward(number)

        @pl.when(here)
        def _():
            local_copy().start()

        @pl.when(jnp.logical_not(here))
        def _():
            remote_copy().start()

        return carry

    lax.fori_loop(0, groups, send, 0)

    def forward(number, carry):
        slot, here, local_copy, remote_copy = along(number)
        landed = relay_ref.at[block(slot), :]
        pltpu.make_async_copy(landed, landed, recv_sem.at[slot]).wait()

        @pl.when(here)
        def _():
            local_copy().start()

        @pl.when(jnp.logical_not(here))
        def _():
            remote_copy().start()

        return carry

    lax.fori_loop(0, groups, forward, 0)

    def drain(source, carry):
        landed = out_ref.at[block(source), :]
        pltpu.make_async_copy(landed, landed, pass_recv.at[source]).wait()
        return carry

    lax.fori_loop(0, groups, drain, 0)

    def sent(number, carry):
        here, _, remote_copy = outward(number)
        _, passed_here, _, passed_copy = along(number)

        @pl.when(jnp.logical_not(here))
        def _():
            remote_copy().wait_send()

        @pl.when(jnp.logical_not(passed_here))
        def _():
            passed_copy().wait_send()

        return carry

    lax.fori_loop(0, groups, sent, 0)


def curvature(total, width):
    gate_pre, up_pre, gate_tan, up_tan, grad_hidden, tan_grad = (
        total[:, width * place : width * (place + 1)] for place in range(6)
    )
    sigmoid_gate = jax.nn.sigmoid(gate_pre)
    silu_gate = gate_pre * sigmoid_gate
    slope = sigmoid_gate * (1.0 + gate_pre * (1.0 - sigmoid_gate))
    bend = sigmoid_gate * (1.0 - sigmoid_gate) * (2.0 + gate_pre * (1.0 - 2.0 * sigmoid_gate))
    tan_gate = (
        tan_grad * up_pre * slope
        + grad_hidden * up_tan * slope
        + grad_hidden * up_pre * bend * gate_tan
    )
    tan_up = tan_grad * silu_gate + grad_hidden * slope * gate_tan
    tan_hidden = slope * gate_tan * up_pre + silu_gate * up_tan
    return jnp.concatenate([tan_gate, tan_up, tan_hidden], axis=1).astype(jnp.bfloat16)


def group_kernel(
    packed_ref, gate_ref, up_ref, gdir_ref, udir_ref, down_ref, ddir_ref,
    tok_ref, cot_ref, curved_ref,
    fwd_ref, bwd_ref, keep_ref, core_out, core_in, chip_keep, chip_out, chip_in,
    load_sem, core_send, core_recv, chip_send, chip_recv, back_send, back_recv, last_send, last_recv,
):
    rows, depth = tok_ref.shape
    chunks, _, wide = curved_ref.shape
    slim = wide // 3
    halved, quarter = rows // 2, rows // 4
    me, side = lax.axis_index("fsdp"), lax.axis_index("tp")
    core, chip = me % 2, (me % 4) // 2
    core_mate = (me + 1 - 2 * core, side)
    chip_mate = (me + 2 - 4 * chip, side)

    def loads(chunk):
        at = slice(chunk * slim, (chunk + 1) * slim)
        pieces = [
            (ref.at[:, at], fwd_ref.at[chunk, :, pl.ds(place * slim, slim)])
            for place, ref in enumerate((gate_ref, up_ref, gdir_ref, udir_ref))
        ] + [
            (ref.at[at, :], bwd_ref.at[chunk, pl.ds(place * slim, slim), :])
            for place, ref in enumerate((down_ref, ddir_ref))
        ]
        return [
            pltpu.make_async_copy(source, target, load_sem.at[chunk, place])
            for place, (source, target) in enumerate(pieces)
        ]

    barrier = pltpu.get_barrier_semaphore()
    for mate in (core_mate, chip_mate):
        pl.semaphore_signal(barrier, inc=1, device_id=mate, device_id_type=MESH)
    for chunk in range(chunks):
        for copy in loads(chunk):
            copy.start()

    sort_rows = 4 * BLOCK
    left = lax.broadcasted_iota(jnp.int32, (sort_rows, 1), 0).astype(jnp.float32)
    source = jnp.floor((left + 0.5) * (1.0 / BLOCK))
    part = jnp.floor((left - source * BLOCK + 0.5) * (1.0 / CAPACITY))
    rest = left - source * BLOCK - part * CAPACITY
    out_part, out_source, out_rest = source, part, rest
    wanted = out_source * BLOCK + out_part * CAPACITY + out_rest
    have = lax.broadcasted_iota(jnp.int32, (1, sort_rows), 1).astype(jnp.float32)
    sorter = jnp.where(wanted == have, 1.0, 0.0).astype(jnp.bfloat16)
    fine = depth // 2

    def sort(group, carry):
        block = packed_ref[pl.ds(pl.multiple_of(group * sort_rows, sort_rows), sort_rows), :]
        ordered = jnp.dot(sorter, block, preferred_element_type=jnp.float32).astype(jnp.bfloat16)
        to = pl.ds(pl.multiple_of(group * BLOCK, BLOCK), BLOCK)
        tok_ref[to, 0:fine] = ordered[0:BLOCK]
        tok_ref[to, fine:depth] = ordered[BLOCK : 2 * BLOCK]
        cot_ref[to, 0:fine] = ordered[2 * BLOCK : 3 * BLOCK]
        cot_ref[to, fine:depth] = ordered[3 * BLOCK : 4 * BLOCK]
        return carry

    lax.fori_loop(0, rows // BLOCK, sort, 0)
    pl.semaphore_wait(barrier, 2)

    against = (((1,), (1,)), ((), ()))

    def to_core(chunk):
        return pltpu.make_async_remote_copy(
            src_ref=core_out.at[chunk], dst_ref=core_in.at[chunk],
            send_sem=core_send.at[chunk], recv_sem=core_recv.at[chunk],
            device_id=core_mate, device_id_type=MESH,
        )

    def to_chip(chunk):
        return pltpu.make_async_remote_copy(
            src_ref=chip_out.at[chunk], dst_ref=chip_in.at[chunk],
            send_sem=chip_send.at[chunk], recv_sem=chip_recv.at[chunk],
            device_id=chip_mate, device_id_type=MESH,
        )

    def back(chunk, where):
        place = curved_ref.at[chunk, pl.ds(pl.multiple_of(where, quarter), quarter), :]
        return pltpu.make_async_remote_copy(
            src_ref=place, dst_ref=place,
            send_sem=back_send.at[chunk], recv_sem=back_recv.at[chunk],
            device_id=chip_mate, device_id_type=MESH,
        )

    def last(chunk, where):
        place = curved_ref.at[chunk, pl.ds(pl.multiple_of(where, halved), halved), :]
        return pltpu.make_async_remote_copy(
            src_ref=place, dst_ref=place,
            send_sem=last_send.at[chunk], recv_sem=last_recv.at[chunk],
            device_id=core_mate, device_id_type=MESH,
        )

    my_half, mate_half = core * halved, (1 - core) * halved
    my_quarter = my_half + chip * quarter
    mate_quarter = my_half + (1 - chip) * quarter

    def forward(chunk, begin, into):
        at = pl.ds(pl.multiple_of(begin, halved), halved)
        into[chunk, :, 0 : 4 * slim] = jnp.dot(
            tok_ref[at, :], fwd_ref[chunk], preferred_element_type=jnp.float32
        )
        into[chunk, :, 4 * slim : 6 * slim] = lax.dot_general(
            cot_ref[at, :], bwd_ref[chunk], against, preferred_element_type=jnp.float32
        )

    def products(chunk):
        for place in range(6):
            pltpu.make_async_copy(
                bwd_ref.at[chunk, pl.ds(0, slim), :] if place >= 4 else fwd_ref.at[chunk, :, pl.ds(0, slim)],
                bwd_ref.at[chunk, pl.ds(0, slim), :] if place >= 4 else fwd_ref.at[chunk, :, pl.ds(0, slim)],
                load_sem.at[chunk, place],
            ).wait()
        forward(chunk, mate_half, core_out)
        to_core(chunk).start()
        forward(chunk, my_half, keep_ref)

    def core_sum(chunk):
        to_core(chunk).wait_recv()
        theirs = pl.ds(pl.multiple_of((1 - chip) * quarter, quarter), quarter)
        chip_out[chunk] = (keep_ref[chunk, theirs, :] + core_in[chunk, theirs, :]).astype(jnp.bfloat16)
        to_chip(chunk).start()
        ours = pl.ds(pl.multiple_of(chip * quarter, quarter), quarter)
        chip_keep[chunk] = keep_ref[chunk, ours, :] + core_in[chunk, ours, :]

    def first_pass(step, carry):
        @pl.when(step < chunks)
        def _():
            products(step)

        @pl.when(step > 0)
        def _():
            core_sum(step - 1)

        return carry

    lax.fori_loop(0, chunks + 1, first_pass, 0)

    def curve(chunk, carry):
        to_chip(chunk).wait_recv()
        total = chip_keep[chunk] + chip_in[chunk].astype(jnp.float32)
        curved_ref[chunk, pl.ds(pl.multiple_of(my_quarter, quarter), quarter), :] = curvature(total, slim)
        back(chunk, my_quarter).start()
        return carry

    lax.fori_loop(0, chunks, curve, 0)

    def spread(chunk, carry):
        back(chunk, mate_quarter).wait_recv()
        last(chunk, my_half).start()
        return carry

    lax.fori_loop(0, chunks, spread, 0)

    def finish(chunk, carry):
        last(chunk, mate_half).wait_recv()
        to_core(chunk).wait_send()
        to_chip(chunk).wait_send()
        back(chunk, my_quarter).wait_send()
        last(chunk, my_half).wait_send()
        return carry

    lax.fori_loop(0, chunks, finish, 0)


def product_kernel(tok_ref, cot_ref, curved_ref, gate_out, up_out, down_out, flipped):
    slim = curved_ref.shape[2] // 3

    @pl.when(pl.program_id(0) == 0)
    def _():
        flipped[...] = tok_ref[...].T

    both = jnp.dot(flipped[...], curved_ref[0, :, 0 : 2 * slim], preferred_element_type=jnp.float32)
    gate_out[...] = both[:, 0:slim]
    up_out[...] = both[:, slim : 2 * slim]
    down_out[...] = lax.dot_general(
        curved_ref[0, :, 2 * slim : 3 * slim],
        cot_ref[...],
        (((0,), (0,)), ((), ())),
        preferred_element_type=jnp.float32,
    )


def local(
    tokens, cotangent, routes, gates, gate_proj, up_proj, down_proj, gate_dir, up_dir, down_dir
):
    count, width = tokens.shape
    groups = lax.axis_size("fsdp")
    experts = groups // 4
    depth, hidden = gate_proj.shape[1:]
    rows = groups * CAPACITY
    slim = 128
    chunks = hidden // slim
    halved, quarter = rows // 2, rows // 4
    bf16, f32 = jnp.bfloat16, jnp.float32

    packed = pl.pallas_call(
        dispatch_kernel,
        name="dispatch",
        out_shape=jax.ShapeDtypeStruct((groups * BLOCK, width // 4), bf16),
        in_specs=[SPACE] * 4,
        out_specs=HBM,
        scratch_shapes=[
            pltpu.VMEM((2, experts * BLOCK, width // 4), bf16),
            pltpu.VMEM((experts * BLOCK, 4 * count), bf16),
            pltpu.VMEM((2, 4 * count, width // 4), bf16),
            pltpu.VMEM((groups * BLOCK, width // 4), bf16),
        ]
        + [pltpu.SemaphoreType.DMA((groups,))] * 4,
        compiler_params=pltpu.CompilerParams(
            collective_id=0, has_side_effects=True, vmem_limit_bytes=VMEM_LIMIT
        ),
    )(tokens, cotangent, routes.reshape(1, count), gates.reshape(1, count))

    tok, cot, curved = pl.pallas_call(
        group_kernel,
        name="group",
        out_shape=(
            jax.ShapeDtypeStruct((rows, depth), bf16),
            jax.ShapeDtypeStruct((rows, depth), bf16),
            jax.ShapeDtypeStruct((chunks, rows, 3 * slim), bf16),
        ),
        in_specs=[SPACE] + [HBM] * 6,
        out_specs=(SPACE,) * 3,
        scratch_shapes=[
            pltpu.VMEM((chunks, depth, 4 * slim), bf16),
            pltpu.VMEM((chunks, 2 * slim, depth), bf16),
            pltpu.VMEM((chunks, halved, 6 * slim), f32),
            pltpu.VMEM((chunks, halved, 6 * slim), f32),
            pltpu.VMEM((chunks, halved, 6 * slim), f32),
            pltpu.VMEM((chunks, quarter, 6 * slim), f32),
            pltpu.VMEM((chunks, quarter, 6 * slim), bf16),
            pltpu.VMEM((chunks, quarter, 6 * slim), bf16),
            pltpu.SemaphoreType.DMA((chunks, 6)),
        ]
        + [pltpu.SemaphoreType.DMA((chunks,))] * 8,
        compiler_params=pltpu.CompilerParams(
            collective_id=1, has_side_effects=True, vmem_limit_bytes=VMEM_LIMIT
        ),
    )(packed, gate_proj[0], up_proj[0], gate_dir[0], up_dir[0], down_proj[0], down_dir[0])

    whole = lambda chunk: (0, 0)
    hess_gate, hess_up, hess_down = pl.pallas_call(
        product_kernel,
        name="products",
        grid=(chunks,),
        out_shape=(
            jax.ShapeDtypeStruct((depth, hidden), f32),
            jax.ShapeDtypeStruct((depth, hidden), f32),
            jax.ShapeDtypeStruct((hidden, depth), f32),
        ),
        in_specs=[
            pl.BlockSpec((rows, depth), whole),
            pl.BlockSpec((rows, depth), whole),
            pl.BlockSpec((1, rows, 3 * slim), lambda chunk: (chunk, 0, 0)),
        ],
        out_specs=(
            pl.BlockSpec((depth, slim), lambda chunk: (0, chunk)),
            pl.BlockSpec((depth, slim), lambda chunk: (0, chunk)),
            pl.BlockSpec((slim, depth), lambda chunk: (chunk, 0)),
        ),
        scratch_shapes=[pltpu.VMEM((depth, rows), bf16)],
        compiler_params=pltpu.CompilerParams(vmem_limit_bytes=VMEM_LIMIT),
    )(tok, cot, curved)
    return (hess_gate[None], hess_up[None], hess_down[None])


def solution(mesh):
    return jax.shard_map(
        local,
        mesh=mesh,
        in_specs=(
            P("fsdp", "tp"),
            P("fsdp", "tp"),
            P("fsdp", None),
            P("fsdp", None),
            P("fsdp", None, "tp"),
            P("fsdp", None, "tp"),
            P("fsdp", "tp", None),
            P("fsdp", None, "tp"),
            P("fsdp", None, "tp"),
            P("fsdp", "tp", None),
        ),
        out_specs=(P("fsdp", None, "tp"), P("fsdp", None, "tp"), P("fsdp", "tp", None)),
        check_vma=False,
    )
```

```python
import jax
import jax.numpy as jnp
from jax import lax
from jax.experimental import pallas as pl
from jax.experimental.pallas import tpu as pltpu
from jax.sharding import PartitionSpec as P

MESH = pl.DeviceIdType.MESH
CAPACITY = 12
BLOCK = 4 * CAPACITY
VMEM_LIMIT = 60 * 1024 * 1024
SPACE = pl.BlockSpec(memory_space=pltpu.VMEM)
HBM = pl.BlockSpec(memory_space=pl.ANY)


def layer_kernel(
    mine_ref, cotan_ref, route_ref, weight_ref, gate_ref, up_ref, gdir_ref, udir_ref, down_ref, ddir_ref,
    flip_ref, cot_ref, curved_ref,
    send_ref, pick_ref, feed_ref, relay_ref, packed_ref, tok_ref,
    fwd_ref, bwd_ref, keep_ref, core_out, core_in, chip_keep, chip_out, chip_in,
    send_sem, recv_sem, pass_send, pass_recv,
    load_sem, core_send, core_recv, chip_send, chip_recv, back_send, back_recv, last_send, last_recv,
):
    tokens, width = mine_ref.shape
    fine = width // 4
    groups = packed_ref.shape[0] // BLOCK
    rows, depth = tok_ref.shape
    chunks, _, wide = curved_ref.shape
    slim = wide // 3
    units = 2 * chunks
    parted, halved, quarter = rows // 2, rows // 4, rows // 8
    experts = groups // 4
    me, high = lax.axis_index("fsdp"), lax.axis_index("tp")
    z, low, x, core = me // 16, (me // 8) % 2, (me // 2) % 4, me % 2
    y = high * 2 + low

    def plane(to_z, to_y):
        return to_z * 16 + (to_y % 2) * 8 + x * 2 + core, to_y // 2

    def beside(to_x, to_core):
        return me - x * 2 - core + to_x * 2 + to_core, high

    barrier = pltpu.get_barrier_semaphore()
    for step in range(1, 16):
        pl.semaphore_signal(
            barrier, inc=1, device_id=plane((z + step // 4) % 4, (y + step % 4) % 4), device_id_type=MESH
        )
    for step in range(1, 8):
        pl.semaphore_signal(
            barrier, inc=1, device_id=beside((x + step // 2) % 4, (core + step) % 2), device_id_type=MESH
        )

    def loads(chunk):
        at = slice(chunk * slim, (chunk + 1) * slim)
        pieces = [
            (ref.at[:, at], fwd_ref.at[chunk, :, pl.ds(place * slim, slim)])
            for place, ref in enumerate((gate_ref, up_ref, gdir_ref, udir_ref))
        ] + [
            (ref.at[at, :], bwd_ref.at[chunk, pl.ds(place * slim, slim), :])
            for place, ref in enumerate((down_ref, ddir_ref))
        ]
        return [
            pltpu.make_async_copy(source, target, load_sem.at[chunk, place])
            for place, (source, target) in enumerate(pieces)
        ]

    row = route_ref[...].astype(jnp.float32)
    col = jnp.broadcast_to(row, (tokens, tokens)).T
    first = lax.broadcasted_iota(jnp.int32, (tokens, tokens), 0)
    second = lax.broadcasted_iota(jnp.int32, (tokens, tokens), 1)
    before = jnp.where((col == row) & (first < second), 1.0, 0.0)
    slot = row * CAPACITY + jnp.sum(before, axis=0, keepdims=True)
    key = jnp.concatenate([slot + 1024.0 * part for part in range(4)], axis=1)
    place = lax.broadcasted_iota(jnp.int32, (experts * BLOCK, 1), 0).astype(jnp.float32)
    expert = jnp.floor((place + 0.5) * (1.0 / BLOCK))
    within = place - expert * BLOCK
    part = jnp.floor((within + 0.5) * (1.0 / CAPACITY))
    wanted = expert * CAPACITY + (within - part * CAPACITY) + 1024.0 * part
    pick_ref[...] = jnp.where(wanted == key, 1.0, 0.0).astype(jnp.bfloat16)
    gate = jnp.broadcast_to(weight_ref[...], (tokens, tokens)).T[:, 0:1]
    weighted = (gate * cotan_ref[...].astype(jnp.float32)).astype(jnp.bfloat16)
    for piece in range(2):
        for side in range(2):
            lanes = slice((2 * piece + side) * fine, (2 * piece + side + 1) * fine)
            feed_ref[piece, pl.ds(side * tokens, tokens), :] = mine_ref[:, lanes]
            feed_ref[piece, pl.ds((2 + side) * tokens, tokens), :] = weighted[:, lanes]

    def gather(step, carry):
        at = pl.ds(pl.multiple_of(step * 4 * BLOCK, 4 * BLOCK), 4 * BLOCK)
        for piece in range(2):
            send_ref[piece, at, :] = jnp.dot(
                pick_ref[at, :], feed_ref[piece], preferred_element_type=jnp.float32
            ).astype(jnp.bfloat16)
        return carry

    lax.fori_loop(0, experts // 4, gather, 0)
    pl.semaphore_wait(barrier, 22)

    def block(number, count=1):
        return pl.ds(pl.multiple_of(number * BLOCK, BLOCK), count * BLOCK)

    def pair_of(stage):
        return (x // 2 + 1 + stage // 2) % 2, (core + stage) % 2

    def moves(number):
        stage, step = number // 16, number % 16
        return stage, step % 4, (step // 4 + step) % 4

    def outward(number):
        stage, dz, dy = moves(number)
        pair, to_core = pair_of(stage)
        to_z, to_y = (z + dz) % 4, (y + dy) % 4
        slot = stage * 16 + z * 4 + y
        source = send_ref.at[to_core, block(to_z * 4 + (to_y % 2) * 2 + pair), :]
        target = relay_ref.at[block(slot), :]
        here = jnp.logical_and(dz == 0, dy == 0)
        local_copy = lambda: pltpu.make_async_copy(source, target, recv_sem.at[slot])
        remote_copy = lambda: pltpu.make_async_remote_copy(
            src_ref=source, dst_ref=target, send_sem=send_sem.at[number], recv_sem=recv_sem.at[slot],
            device_id=plane(to_z, to_y), device_id_type=MESH,
        )
        return here, local_copy, remote_copy

    def along(number):
        stage, dz, dy = moves(number)
        pair, to_core = pair_of(stage)
        from_z, from_y = (z + 4 - dz) % 4, (y + 4 - dy) % 4
        slot = stage * 16 + from_z * 4 + from_y
        origin = (stage // 2) * 32 + from_z * 8 + (from_y % 2) * 4 + (x % 2) * 2 + core
        to_x = pair * 2 + from_y // 2
        source, target = relay_ref.at[block(slot), :], packed_ref.at[block(origin), :]
        here = jnp.logical_and(to_x == x, to_core == core)
        local_copy = lambda: pltpu.make_async_copy(source, target, pass_recv.at[origin])
        remote_copy = lambda: pltpu.make_async_remote_copy(
            src_ref=source, dst_ref=target, send_sem=pass_send.at[number], recv_sem=pass_recv.at[origin],
            device_id=beside(to_x, to_core), device_id_type=MESH,
        )
        return slot, here, local_copy, remote_copy

    def send(number, carry):
        here, local_copy, remote_copy = outward(number)

        @pl.when(here)
        def _():
            local_copy().start()

        @pl.when(jnp.logical_not(here))
        def _():
            remote_copy().start()

        return carry

    lax.fori_loop(0, groups, send, 0)
    for chunk in range(chunks):
        for copy in loads(chunk):
            copy.start()

    def forward(number, carry):
        slot, here, local_copy, remote_copy = along(number)
        landed = relay_ref.at[block(slot), :]
        pltpu.make_async_copy(landed, landed, recv_sem.at[slot]).wait()

        @pl.when(here)
        def _():
            local_copy().start()

        @pl.when(jnp.logical_not(here))
        def _():
            remote_copy().start()

        return carry

    lax.fori_loop(0, groups, forward, 0)

    sort_rows = 4 * BLOCK
    left = lax.broadcasted_iota(jnp.int32, (sort_rows, 1), 0).astype(jnp.float32)
    part = jnp.floor((left + 0.5) * (1.0 / BLOCK))
    source = jnp.floor((left - part * BLOCK + 0.5) * (1.0 / CAPACITY))
    rest = left - part * BLOCK - source * CAPACITY
    wanted = source * BLOCK + part * CAPACITY + rest
    have = lax.broadcasted_iota(jnp.int32, (1, sort_rows), 1).astype(jnp.float32)
    sorter = jnp.where(wanted == have, 1.0, 0.0).astype(jnp.bfloat16)

    def sort(group, carry):
        for number in range(4):
            landed = packed_ref.at[block(group * 4 + number), :]
            pltpu.make_async_copy(landed, landed, pass_recv.at[group * 4 + number]).wait()
        taken = packed_ref[pl.ds(pl.multiple_of(group * sort_rows, sort_rows), sort_rows), :]
        ordered = jnp.dot(sorter, taken, preferred_element_type=jnp.float32).astype(jnp.bfloat16)
        to = pl.ds(pl.multiple_of(group * BLOCK, BLOCK), BLOCK)
        tok_ref[to, 0:fine] = ordered[0:BLOCK]
        tok_ref[to, fine:depth] = ordered[BLOCK : 2 * BLOCK]
        cot_ref[to, 0:fine] = ordered[2 * BLOCK : 3 * BLOCK]
        cot_ref[to, fine:depth] = ordered[3 * BLOCK : 4 * BLOCK]
        return carry


    against = (((1,), (1,)), ((), ()))

    chip = x % 2
    core_mate, chip_mate = beside(x, 1 - core), beside(x + 1 - 2 * chip, core)

    def to_core(unit):
        slot = unit % 4
        return pltpu.make_async_remote_copy(
            src_ref=core_out.at[slot], dst_ref=core_in.at[unit],
            send_sem=core_send.at[unit], recv_sem=core_recv.at[unit],
            device_id=core_mate, device_id_type=MESH,
        )

    def to_chip(unit):
        return pltpu.make_async_remote_copy(
            src_ref=chip_out.at[unit], dst_ref=chip_in.at[unit],
            send_sem=chip_send.at[unit], recv_sem=chip_recv.at[unit],
            device_id=chip_mate, device_id_type=MESH,
        )

    def back(unit, where):
        begin = unit // chunks * parted + core * halved + where * quarter
        place = curved_ref.at[unit % chunks, pl.ds(pl.multiple_of(begin, quarter), quarter), :]
        return pltpu.make_async_remote_copy(
            src_ref=place, dst_ref=place,
            send_sem=back_send.at[unit], recv_sem=back_recv.at[unit],
            device_id=chip_mate, device_id_type=MESH,
        )

    def last(unit, where):
        begin = unit // chunks * parted + where * halved
        place = curved_ref.at[unit % chunks, pl.ds(pl.multiple_of(begin, halved), halved), :]
        return pltpu.make_async_remote_copy(
            src_ref=place, dst_ref=place,
            send_sem=last_send.at[unit], recv_sem=last_recv.at[unit],
            device_id=core_mate, device_id_type=MESH,
        )

    def forward_products(unit, whose, into, slot):
        chunk = unit % chunks
        begin = unit // chunks * parted + whose * halved
        at = pl.ds(pl.multiple_of(begin, halved), halved)
        into[slot, :, 0 : 4 * slim] = jnp.dot(
            tok_ref[at, :], fwd_ref[chunk], preferred_element_type=jnp.float32
        )
        into[slot, :, 4 * slim : 6 * slim] = lax.dot_general(
            cot_ref[at, :], bwd_ref[chunk], against, preferred_element_type=jnp.float32
        )

    def products(unit):
        @pl.when(unit < chunks)
        def _():
            for place in range(6):
                loaded = (
                    bwd_ref.at[unit, pl.ds(0, slim), :] if place >= 4 else fwd_ref.at[unit, :, pl.ds(0, slim)]
                )
                pltpu.make_async_copy(loaded, loaded, load_sem.at[unit, place]).wait()

        @pl.when(unit >= 4)
        def _():
            to_core(unit - 4).wait_send()

        forward_products(unit, 1 - core, core_out, unit % 4)
        to_core(unit).start()
        forward_products(unit, core, keep_ref, unit % 2)

    def core_sum(unit):
        to_core(unit).wait_recv()
        slot = unit % 2
        theirs = pl.ds(pl.multiple_of((1 - chip) * quarter, quarter), quarter)
        chip_out[unit] = (keep_ref[slot, theirs, :] + core_in[unit, theirs, :]).astype(jnp.bfloat16)
        to_chip(unit).start()
        ours = pl.ds(pl.multiple_of(chip * quarter, quarter), quarter)
        chip_keep[unit] = keep_ref[slot, ours, :] + core_in[unit, ours, :]

    def first_pass(step, carry):
        @pl.when(step % chunks == 0)
        def _():
            @pl.when(step < units)
            def _():
                lax.fori_loop(step // chunks * 8, step // chunks * 8 + 8, sort, 0)

        @pl.when(step < units)
        def _():
            products(step)

        @pl.when(step > 0)
        def _():
            core_sum(step - 1)

        return carry

    lax.fori_loop(0, units + 1, first_pass, 0)
    flip_ref[...] = tok_ref[...].T

    def curve(unit, carry):
        to_chip(unit).wait_recv()
        total = chip_keep[unit] + chip_in[unit].astype(jnp.float32)
        begin = unit // chunks * parted + core * halved + chip * quarter
        curved_ref[unit % chunks, pl.ds(pl.multiple_of(begin, quarter), quarter), :] = curvature(total, slim)
        back(unit, chip).start()
        return carry

    lax.fori_loop(0, units, curve, 0)

    def spread(unit, carry):
        back(unit, 1 - chip).wait_recv()
        last(unit, core).start()
        return carry

    lax.fori_loop(0, units, spread, 0)

    def finish(unit, carry):
        last(unit, 1 - core).wait_recv()

        @pl.when(unit >= units - 4)
        def _():
            to_core(unit).wait_send()

        to_chip(unit).wait_send()
        back(unit, chip).wait_send()
        last(unit, core).wait_send()
        return carry

    lax.fori_loop(0, units, finish, 0)
    def sent(number, carry):
        here, _, remote_copy = outward(number)
        _, passed_here, _, passed_copy = along(number)

        @pl.when(jnp.logical_not(here))
        def _():
            remote_copy().wait_send()

        @pl.when(jnp.logical_not(passed_here))
        def _():
            passed_copy().wait_send()

        return carry

    lax.fori_loop(0, groups, sent, 0)


def curvature(total, width):
    gate_pre, up_pre, gate_tan, up_tan, grad_hidden, tan_grad = (
        total[:, width * place : width * (place + 1)] for place in range(6)
    )
    sigmoid_gate = jax.nn.sigmoid(gate_pre)
    silu_gate = gate_pre * sigmoid_gate
    slope = sigmoid_gate * (1.0 + gate_pre * (1.0 - sigmoid_gate))
    bend = sigmoid_gate * (1.0 - sigmoid_gate) * (2.0 + gate_pre * (1.0 - 2.0 * sigmoid_gate))
    tan_gate = (
        tan_grad * up_pre * slope
        + grad_hidden * up_tan * slope
        + grad_hidden * up_pre * bend * gate_tan
    )
    tan_up = tan_grad * silu_gate + grad_hidden * slope * gate_tan
    tan_hidden = slope * gate_tan * up_pre + silu_gate * up_tan
    return jnp.concatenate([tan_gate, tan_up, tan_hidden], axis=1).astype(jnp.bfloat16)


def product_kernel(flip_ref, cot_ref, curved_ref, gate_out, up_out, down_out):
    slim = curved_ref.shape[2] // 3

    both = jnp.dot(flip_ref[...], curved_ref[0, :, 0 : 2 * slim], preferred_element_type=jnp.float32)
    gate_out[...] = both[:, 0:slim]
    up_out[...] = both[:, slim : 2 * slim]
    down_out[...] = lax.dot_general(
        curved_ref[0, :, 2 * slim : 3 * slim],
        cot_ref[...],
        (((0,), (0,)), ((), ())),
        preferred_element_type=jnp.float32,
    )


def local(
    tokens, cotangent, routes, gates, gate_proj, up_proj, down_proj, gate_dir, up_dir, down_dir
):
    count, width = tokens.shape
    groups = lax.axis_size("fsdp")
    experts = groups // 4
    depth, hidden = gate_proj.shape[1:]
    rows = groups * CAPACITY
    slim = 128
    chunks = hidden // slim
    bf16, f32 = jnp.bfloat16, jnp.float32

    units = 2 * chunks
    flipped, cot, curved = pl.pallas_call(
        layer_kernel,
        name="layer",
        out_shape=(
            jax.ShapeDtypeStruct((depth, rows), bf16),
            jax.ShapeDtypeStruct((rows, depth), bf16),
            jax.ShapeDtypeStruct((chunks, rows, 3 * slim), bf16),
        ),
        in_specs=[SPACE] * 4 + [HBM] * 6,
        out_specs=(SPACE,) * 3,
        scratch_shapes=[
            pltpu.VMEM((2, experts * BLOCK, width // 4), bf16),
            pltpu.VMEM((experts * BLOCK, 4 * count), bf16),
            pltpu.VMEM((2, 4 * count, width // 4), bf16),
            pltpu.VMEM((groups * BLOCK, width // 4), bf16),
            pltpu.VMEM((groups * BLOCK, width // 4), bf16),
            pltpu.VMEM((rows, depth), bf16),
            pltpu.VMEM((chunks, depth, 4 * slim), bf16),
            pltpu.VMEM((chunks, 2 * slim, depth), bf16),
            pltpu.VMEM((2, rows // 4, 6 * slim), f32),
            pltpu.VMEM((4, rows // 4, 6 * slim), f32),
            pltpu.VMEM((units, rows // 4, 6 * slim), f32),
            pltpu.VMEM((units, rows // 8, 6 * slim), f32),
            pltpu.VMEM((units, rows // 8, 6 * slim), bf16),
            pltpu.VMEM((units, rows // 8, 6 * slim), bf16),
        ]
        + [pltpu.SemaphoreType.DMA((groups,))] * 4
        + [pltpu.SemaphoreType.DMA((chunks, 6))]
        + [pltpu.SemaphoreType.DMA((units,))] * 8,
        compiler_params=pltpu.CompilerParams(
            collective_id=0, has_side_effects=True, vmem_limit_bytes=VMEM_LIMIT
        ),
    )(
        tokens, cotangent, routes.reshape(1, count), gates.reshape(1, count),
        gate_proj[0], up_proj[0], gate_dir[0], up_dir[0], down_proj[0], down_dir[0],
    )

    whole = lambda chunk: (0, 0)
    hess_gate, hess_up, hess_down = pl.pallas_call(
        product_kernel,
        name="products",
        grid=(chunks,),
        out_shape=(
            jax.ShapeDtypeStruct((depth, hidden), f32),
            jax.ShapeDtypeStruct((depth, hidden), f32),
            jax.ShapeDtypeStruct((hidden, depth), f32),
        ),
        in_specs=[
            pl.BlockSpec((depth, rows), whole),
            pl.BlockSpec((rows, depth), whole),
            pl.BlockSpec((1, rows, 3 * slim), lambda chunk: (chunk, 0, 0)),
        ],
        out_specs=(
            pl.BlockSpec((depth, slim), lambda chunk: (0, chunk)),
            pl.BlockSpec((depth, slim), lambda chunk: (0, chunk)),
            pl.BlockSpec((slim, depth), lambda chunk: (chunk, 0)),
        ),
        compiler_params=pltpu.CompilerParams(vmem_limit_bytes=VMEM_LIMIT),
    )(flipped, cot, curved)
    return (hess_gate[None], hess_up[None], hess_down[None])


def solution(mesh):
    return jax.shard_map(
        local,
        mesh=mesh,
        in_specs=(
            P("fsdp", "tp"),
            P("fsdp", "tp"),
            P("fsdp", None),
            P("fsdp", None),
            P("fsdp", None, "tp"),
            P("fsdp", None, "tp"),
            P("fsdp", "tp", None),
            P("fsdp", None, "tp"),
            P("fsdp", None, "tp"),
            P("fsdp", "tp", None),
        ),
        out_specs=(P("fsdp", None, "tp"), P("fsdp", None, "tp"), P("fsdp", "tp", None)),
        check_vma=False,
    )
```

```python
import jax
import jax.numpy as jnp
from jax import lax
from jax.experimental import pallas as pl
from jax.experimental.pallas import tpu as pltpu
from jax.sharding import PartitionSpec as P

MESH = pl.DeviceIdType.MESH
CAPACITY = 12
BLOCK = 4 * CAPACITY
VMEM_LIMIT = 60 * 1024 * 1024
SPACE = pl.BlockSpec(memory_space=pltpu.VMEM)
HBM = pl.BlockSpec(memory_space=pl.ANY)


def layer_kernel(
    mine_ref, cotan_ref, route_ref, weight_ref, gate_ref, up_ref, gdir_ref, udir_ref, down_ref, ddir_ref,
    flip_ref, cot_ref, curved_ref,
    send_ref, pick_ref, feed_ref, first_ref, second_ref, packed_ref, tok_ref,
    fwd_ref, bwd_ref, part_ref, core_in, chip_keep, chip_out, chip_in,
    z_send, z_recv, x_send, x_recv, y_send, y_recv,
    load_sem, core_send, core_recv, chip_send, chip_recv, back_send, back_recv, last_send, last_recv,
):
    tokens, width = mine_ref.shape
    fine = width // 4
    rows, depth = tok_ref.shape
    chunks, _, wide = curved_ref.shape
    slim = wide // 3
    parts = packed_ref.shape[0] // 4
    units = parts * chunks
    parted, halved, quarter = rows // parts, rows // parts // 2, rows // parts // 4
    experts = 4 * parts
    me, high = lax.axis_index("fsdp"), lax.axis_index("tp")
    z, low, x, core = me // 16, (me // 8) % 2, (me // 2) % 4, me % 2
    y = high * 2 + low
    facing = y + core * (3 - 2 * y)

    def plane(to_z, to_y):
        return to_z * 16 + (to_y % 2) * 8 + x * 2 + core, to_y // 2

    def beside(to_x, to_core):
        return me - x * 2 - core + to_x * 2 + to_core, high

    barrier = pltpu.get_barrier_semaphore()
    for step in range(1, 4):
        for there in (plane((z + step) % 4, facing), plane(z, (y + step) % 4)):
            pl.semaphore_signal(barrier, inc=1, device_id=there, device_id_type=MESH)
    for step in range(1, 8):
        pl.semaphore_signal(
            barrier, inc=1, device_id=beside((x + step // 2) % 4, (core + step) % 2), device_id_type=MESH
        )

    def loads(chunk):
        at = slice(chunk * slim, (chunk + 1) * slim)
        pieces = [
            (ref.at[:, at], fwd_ref.at[chunk, :, pl.ds(place * slim, slim)])
            for place, ref in enumerate((gate_ref, up_ref, gdir_ref, udir_ref))
        ] + [
            (ref.at[at, :], bwd_ref.at[chunk, pl.ds(place * slim, slim), :])
            for place, ref in enumerate((down_ref, ddir_ref))
        ]
        return [
            pltpu.make_async_copy(source, target, load_sem.at[chunk, place])
            for place, (source, target) in enumerate(pieces)
        ]

    row = route_ref[...].astype(jnp.float32)
    col = jnp.broadcast_to(row, (tokens, tokens)).T
    first = lax.broadcasted_iota(jnp.int32, (tokens, tokens), 0)
    second = lax.broadcasted_iota(jnp.int32, (tokens, tokens), 1)
    before = jnp.where((col == row) & (first < second), 1.0, 0.0)
    slot = row * CAPACITY + jnp.sum(before, axis=0, keepdims=True)
    key = jnp.concatenate([slot + 1024.0 * part for part in range(4)], axis=1)
    place = lax.broadcasted_iota(jnp.int32, (experts * BLOCK, 1), 0).astype(jnp.float32)
    number = jnp.floor((place + 0.5) * (1.0 / BLOCK))
    within = place - number * BLOCK
    span = jnp.floor((number + 0.5) * 0.25)
    pair = jnp.floor((number - 4.0 * span + 0.5) * 0.5)
    expert = 2.0 * number - 4.0 * span - 3.0 * pair
    part = jnp.floor((within + 0.5) * (1.0 / CAPACITY))
    wanted = expert * CAPACITY + (within - part * CAPACITY) + 1024.0 * part
    pick_ref[...] = jnp.where(wanted == key, 1.0, 0.0).astype(jnp.bfloat16)
    gate = jnp.broadcast_to(weight_ref[...], (tokens, tokens)).T[:, 0:1]
    weighted = (gate * cotan_ref[...].astype(jnp.float32)).astype(jnp.bfloat16)
    for piece in range(2):
        for side in range(2):
            lanes = slice((2 * piece + side) * fine, (2 * piece + side + 1) * fine)
            feed_ref[piece, pl.ds(side * tokens, tokens), :] = mine_ref[:, lanes]
            feed_ref[piece, pl.ds((2 + side) * tokens, tokens), :] = weighted[:, lanes]

    def gather(step, carry):
        at = pl.ds(pl.multiple_of(step * 4 * BLOCK, 4 * BLOCK), 4 * BLOCK)
        for piece in range(2):
            picked = jnp.dot(pick_ref[at, :], feed_ref[piece], preferred_element_type=jnp.float32)
            for place in range(4):
                send_ref[piece, step, place // 2, place % 2] = picked[
                    place * BLOCK : (place + 1) * BLOCK
                ].astype(jnp.bfloat16)
        return carry

    lax.fori_loop(0, parts, gather, 0)
    pl.semaphore_wait(barrier, 13)

    def transfer(here, source, target, send_sem, recv_sem, device):
        def start():
            @pl.when(here)
            def _():
                pltpu.make_async_copy(source, target, recv_sem).start()

            @pl.when(jnp.logical_not(here))
            def _():
                remote().start()

        def remote():
            return pltpu.make_async_remote_copy(
                src_ref=source, dst_ref=target, send_sem=send_sem, recv_sem=recv_sem,
                device_id=device, device_id_type=MESH,
            )

        def finish():
            @pl.when(jnp.logical_not(here))
            def _():
                remote().wait_send()

        return start, finish

    def landed(place, sem):
        pltpu.make_async_copy(place, place, sem).wait()

    def along_z(part, to_core):
        dz = part + part // 2 * (1 - 2 * (part % 2))
        to_z = (z + dz) % 4
        return transfer(
            jnp.logical_and(dz == 0, core == 0), send_ref.at[to_core, to_z], first_ref.at[part, to_core],
            z_send.at[part * 2 + to_core], z_recv.at[part * 2 + to_core], plane(to_z, facing),
        )

    def along_x(part, pair, to_core):
        to_x = pair * 2 + (high + core) % 2
        return transfer(
            jnp.logical_and(to_x == x, to_core == core),
            first_ref.at[part, to_core, pair],
            second_ref.at[part, :, pl.ds(pl.multiple_of(x * BLOCK, BLOCK), BLOCK), :],
            x_send.at[part * 4 + pair * 2 + to_core], x_recv.at[part * 4 + x], beside(to_x, to_core),
        )

    def along_y(part, to_low, to_high):
        to_y = to_high * 2 + to_low
        origin_core = (high + x) % 2
        origin = (low + origin_core * (1 - 2 * low)) * 2 + origin_core
        return transfer(
            to_y == y, second_ref.at[part, to_low], packed_ref.at[part * 4 + origin],
            y_send.at[part * 4 + to_y], y_recv.at[part * 4 + origin], plane(z, to_y),
        )

    def hop_z(part, carry):
        for to_core in range(2):
            along_z(part, to_core)[0]()
        return carry

    def hop_x(part):
        for to_core in range(2):
            landed(first_ref.at[part, to_core], z_recv.at[part * 2 + to_core])
        for pair in range(2):
            for to_core in range(2):
                along_x(part, pair, to_core)[0]()

    def hop_y(part):
        for number in range(4):
            landed(second_ref.at[part, :, pl.ds(number * BLOCK, BLOCK), :], x_recv.at[part * 4 + number])
        for to_low in range(2):
            for to_high in range(2):
                along_y(part, to_low, to_high)[0]()

    lax.fori_loop(0, parts, hop_z, 0)
    for chunk in range(chunks):
        for copy in loads(chunk):
            copy.start()

    sort_rows = 4 * BLOCK
    left = lax.broadcasted_iota(jnp.int32, (sort_rows, 1), 0).astype(jnp.float32)
    part = jnp.floor((left + 0.5) * (1.0 / BLOCK))
    source = jnp.floor((left - part * BLOCK + 0.5) * (1.0 / CAPACITY))
    rest = left - part * BLOCK - source * CAPACITY
    wanted = source * BLOCK + part * CAPACITY + rest
    have = lax.broadcasted_iota(jnp.int32, (1, sort_rows), 1).astype(jnp.float32)
    sorter = jnp.where(wanted == have, 1.0, 0.0).astype(jnp.bfloat16)

    def sort(group, carry):
        landed(packed_ref.at[group], y_recv.at[group])
        taken = packed_ref[group]
        ordered = jnp.dot(sorter, taken, preferred_element_type=jnp.float32).astype(jnp.bfloat16)
        to = pl.ds(pl.multiple_of(group * BLOCK, BLOCK), BLOCK)
        tok_ref[to, 0:fine] = ordered[0:BLOCK]
        tok_ref[to, fine:depth] = ordered[BLOCK : 2 * BLOCK]
        cot_ref[to, 0:fine] = ordered[2 * BLOCK : 3 * BLOCK]
        cot_ref[to, fine:depth] = ordered[3 * BLOCK : 4 * BLOCK]
        return carry


    against = (((1,), (1,)), ((), ()))

    chip = x % 2
    core_mate, chip_mate = beside(x, 1 - core), beside(x + 1 - 2 * chip, core)

    def to_core(unit):
        theirs = pl.ds(pl.multiple_of((1 - core) * halved, halved), halved)
        return pltpu.make_async_remote_copy(
            src_ref=part_ref.at[unit % 4, theirs, :], dst_ref=core_in.at[unit],
            send_sem=core_send.at[unit], recv_sem=core_recv.at[unit],
            device_id=core_mate, device_id_type=MESH,
        )

    def to_chip(unit):
        return pltpu.make_async_remote_copy(
            src_ref=chip_out.at[unit], dst_ref=chip_in.at[unit],
            send_sem=chip_send.at[unit], recv_sem=chip_recv.at[unit],
            device_id=chip_mate, device_id_type=MESH,
        )

    def back(unit, where):
        begin = unit // chunks * parted + core * halved + where * quarter
        place = curved_ref.at[unit % chunks, pl.ds(pl.multiple_of(begin, quarter), quarter), :]
        return pltpu.make_async_remote_copy(
            src_ref=place, dst_ref=place,
            send_sem=back_send.at[unit], recv_sem=back_recv.at[unit],
            device_id=chip_mate, device_id_type=MESH,
        )

    def last(unit, where):
        begin = unit // chunks * parted + where * halved
        place = curved_ref.at[unit % chunks, pl.ds(pl.multiple_of(begin, halved), halved), :]
        return pltpu.make_async_remote_copy(
            src_ref=place, dst_ref=place,
            send_sem=last_send.at[unit], recv_sem=last_recv.at[unit],
            device_id=core_mate, device_id_type=MESH,
        )

    def products(unit):
        @pl.when(unit < chunks)
        def _():
            for place in range(6):
                loaded = (
                    bwd_ref.at[unit, pl.ds(0, slim), :] if place >= 4 else fwd_ref.at[unit, :, pl.ds(0, slim)]
                )
                pltpu.make_async_copy(loaded, loaded, load_sem.at[unit, place]).wait()

        @pl.when(unit >= 4)
        def _():
            to_core(unit - 4).wait_send()

        chunk = unit % chunks
        at = pl.ds(pl.multiple_of(unit // chunks * parted, parted), parted)
        part_ref[unit % 4, :, 0 : 4 * slim] = jnp.dot(
            tok_ref[at, :], fwd_ref[chunk], preferred_element_type=jnp.float32
        )
        part_ref[unit % 4, :, 4 * slim : 6 * slim] = lax.dot_general(
            cot_ref[at, :], bwd_ref[chunk], against, preferred_element_type=jnp.float32
        )
        to_core(unit).start()

    def core_sum(unit):
        to_core(unit).wait_recv()
        slot = unit % 4

        def whole(where):
            own = pl.ds(pl.multiple_of(core * halved + where * quarter, quarter), quarter)
            return part_ref[slot, own, :] + core_in[unit, pl.ds(pl.multiple_of(where * quarter, quarter), quarter), :]

        chip_out[unit] = whole(1 - chip).astype(jnp.bfloat16)
        to_chip(unit).start()
        chip_keep[unit] = whole(chip)

    def partial_products(part):
        lax.fori_loop(part * 4, part * 4 + 4, sort, 0)

        def both(step, carry):
            @pl.when(step < chunks)
            def _():
                products(part * chunks + step)

            @pl.when(step > 0)
            def _():
                core_sum(part * chunks + step - 1)

            return carry

        lax.fori_loop(0, chunks + 1, both, 0)

    def curve(unit, carry):
        to_chip(unit).wait_recv()
        total = chip_keep[unit] + chip_in[unit].astype(jnp.float32)
        begin = unit // chunks * parted + core * halved + chip * quarter
        curved_ref[unit % chunks, pl.ds(pl.multiple_of(begin, quarter), quarter), :] = curvature(total, slim)
        back(unit, chip).start()
        return carry

    def advance(step, carry):
        @pl.when(step < parts)
        def _():
            hop_x(step)

        @pl.when(jnp.logical_and(step >= 1, step < parts + 1))
        def _():
            hop_y(step - 1)

        @pl.when(jnp.logical_and(step >= 3, step < parts + 3))
        def _():
            partial_products(step - 3)

        @pl.when(step >= 4)
        def _():
            lax.fori_loop((step - 4) * chunks, (step - 3) * chunks, curve, 0)

        return carry

    lax.fori_loop(0, parts + 4, advance, 0)
    flip_ref[...] = tok_ref[...].T

    def spread(unit, carry):
        back(unit, 1 - chip).wait_recv()
        last(unit, core).start()
        return carry

    lax.fori_loop(0, units, spread, 0)

    def finish(unit, carry):
        last(unit, 1 - core).wait_recv()

        @pl.when(unit >= units - 4)
        def _():
            to_core(unit).wait_send()

        to_chip(unit).wait_send()
        back(unit, chip).wait_send()
        last(unit, core).wait_send()
        return carry

    lax.fori_loop(0, units, finish, 0)
    def sent(part, carry):
        for first in range(2):
            along_z(part, first)[1]()
            for second in range(2):
                along_x(part, first, second)[1]()
                along_y(part, first, second)[1]()
        return carry

    lax.fori_loop(0, parts, sent, 0)


def curvature(total, width):
    gate_pre, up_pre, gate_tan, up_tan, grad_hidden, tan_grad = (
        total[:, width * place : width * (place + 1)] for place in range(6)
    )
    sigmoid_gate = jax.nn.sigmoid(gate_pre)
    silu_gate = gate_pre * sigmoid_gate
    slope = sigmoid_gate * (1.0 + gate_pre * (1.0 - sigmoid_gate))
    bend = sigmoid_gate * (1.0 - sigmoid_gate) * (2.0 + gate_pre * (1.0 - 2.0 * sigmoid_gate))
    tan_gate = (
        tan_grad * up_pre * slope
        + grad_hidden * up_tan * slope
        + grad_hidden * up_pre * bend * gate_tan
    )
    tan_up = tan_grad * silu_gate + grad_hidden * slope * gate_tan
    tan_hidden = slope * gate_tan * up_pre + silu_gate * up_tan
    return jnp.concatenate([tan_gate, tan_up, tan_hidden], axis=1).astype(jnp.bfloat16)


def product_kernel(flip_ref, cot_ref, curved_ref, gate_out, up_out, down_out):
    slim = curved_ref.shape[2] // 3

    both = jnp.dot(flip_ref[...], curved_ref[0, :, 0 : 2 * slim], preferred_element_type=jnp.float32)
    gate_out[...] = both[:, 0:slim]
    up_out[...] = both[:, slim : 2 * slim]
    down_out[...] = lax.dot_general(
        curved_ref[0, :, 2 * slim : 3 * slim],
        cot_ref[...],
        (((0,), (0,)), ((), ())),
        preferred_element_type=jnp.float32,
    )


def local(
    tokens, cotangent, routes, gates, gate_proj, up_proj, down_proj, gate_dir, up_dir, down_dir
):
    count, width = tokens.shape
    groups = lax.axis_size("fsdp")
    experts = groups // 4
    depth, hidden = gate_proj.shape[1:]
    rows = groups * CAPACITY
    slim = 256
    chunks = hidden // slim
    bf16, f32 = jnp.bfloat16, jnp.float32

    parts = 4
    units = parts * chunks
    parted = rows // parts
    flipped, cot, curved = pl.pallas_call(
        layer_kernel,
        name="layer",
        out_shape=(
            jax.ShapeDtypeStruct((depth, rows), bf16),
            jax.ShapeDtypeStruct((rows, depth), bf16),
            jax.ShapeDtypeStruct((chunks, rows, 3 * slim), bf16),
        ),
        in_specs=[SPACE] * 4 + [HBM] * 6,
        out_specs=(SPACE,) * 3,
        scratch_shapes=[
            pltpu.VMEM((2, 4, 2, 2, BLOCK, width // 4), bf16),
            pltpu.VMEM((experts * BLOCK, 4 * count), bf16),
            pltpu.VMEM((2, 4 * count, width // 4), bf16),
            pltpu.VMEM((parts, 2, 2, 2, BLOCK, width // 4), bf16),
            pltpu.VMEM((parts, 2, 4 * BLOCK, width // 4), bf16),
            pltpu.VMEM((parts * 4, 4 * BLOCK, width // 4), bf16),
            pltpu.VMEM((rows, depth), bf16),
            pltpu.VMEM((chunks, depth, 4 * slim), bf16),
            pltpu.VMEM((chunks, 2 * slim, depth), bf16),
            pltpu.VMEM((4, parted, 6 * slim), f32),
            pltpu.VMEM((units, parted // 2, 6 * slim), f32),
            pltpu.VMEM((units, parted // 4, 6 * slim), f32),
            pltpu.VMEM((units, parted // 4, 6 * slim), bf16),
            pltpu.VMEM((units, parted // 4, 6 * slim), bf16),
        ]
        + [pltpu.SemaphoreType.DMA((parts * 2,))] * 2
        + [pltpu.SemaphoreType.DMA((parts * 4,))] * 4
        + [pltpu.SemaphoreType.DMA((chunks, 6))]
        + [pltpu.SemaphoreType.DMA((units,))] * 8,
        compiler_params=pltpu.CompilerParams(
            collective_id=0, has_side_effects=True, vmem_limit_bytes=VMEM_LIMIT
        ),
    )(
        tokens, cotangent, routes.reshape(1, count), gates.reshape(1, count),
        gate_proj[0], up_proj[0], gate_dir[0], up_dir[0], down_proj[0], down_dir[0],
    )

    whole = lambda chunk: (0, 0)
    hess_gate, hess_up, hess_down = pl.pallas_call(
        product_kernel,
        name="products",
        grid=(chunks,),
        out_shape=(
            jax.ShapeDtypeStruct((depth, hidden), f32),
            jax.ShapeDtypeStruct((depth, hidden), f32),
            jax.ShapeDtypeStruct((hidden, depth), f32),
        ),
        in_specs=[
            pl.BlockSpec((depth, rows), whole),
            pl.BlockSpec((rows, depth), whole),
            pl.BlockSpec((1, rows, 3 * slim), lambda chunk: (chunk, 0, 0)),
        ],
        out_specs=(
            pl.BlockSpec((depth, slim), lambda chunk: (0, chunk)),
            pl.BlockSpec((depth, slim), lambda chunk: (0, chunk)),
            pl.BlockSpec((slim, depth), lambda chunk: (chunk, 0)),
        ),
        compiler_params=pltpu.CompilerParams(vmem_limit_bytes=VMEM_LIMIT),
    )(flipped, cot, curved)
    return (hess_gate[None], hess_up[None], hess_down[None])


def solution(mesh):
    return jax.shard_map(
        local,
        mesh=mesh,
        in_specs=(
            P("fsdp", "tp"),
            P("fsdp", "tp"),
            P("fsdp", None),
            P("fsdp", None),
            P("fsdp", None, "tp"),
            P("fsdp", None, "tp"),
            P("fsdp", "tp", None),
            P("fsdp", None, "tp"),
            P("fsdp", None, "tp"),
            P("fsdp", "tp", None),
        ),
        out_specs=(P("fsdp", None, "tp"), P("fsdp", None, "tp"), P("fsdp", "tp", None)),
        check_vma=False,
    )
```

```python
import jax
import jax.numpy as jnp
from jax import lax
from jax.experimental import pallas as pl
from jax.experimental.pallas import tpu as pltpu
from jax.sharding import PartitionSpec as P

MESH = pl.DeviceIdType.MESH
CAPACITY = 12
BLOCK = 4 * CAPACITY
VMEM_LIMIT = 60 * 1024 * 1024
SPACE = pl.BlockSpec(memory_space=pltpu.VMEM)
HBM = pl.BlockSpec(memory_space=pl.ANY)


def layer_kernel(
    mine_ref, cotan_ref, route_ref, weight_ref, gate_ref, up_ref, gdir_ref, udir_ref, down_ref, ddir_ref,
    flip_out, cot_out, curved_out,
    flip_ref, cot_ref, curved_ref, send_ref, pick_ref, feed_ref, first_ref, second_ref, packed_ref, tok_ref,
    fwd_ref, bwd_ref, part_ref, core_in, chip_keep, chip_out, chip_in,
    z_send, z_recv, x_send, x_recv, y_send, y_recv,
    load_sem, core_send, core_recv, chip_send, chip_recv, back_send, back_recv, last_send, last_recv, out_sem,
):
    tokens, width = mine_ref.shape
    fine = width // 4
    rows, depth = tok_ref.shape
    chunks, _, wide = curved_ref.shape
    slim = wide // 3
    parts = packed_ref.shape[0] // 4
    units = parts * chunks
    parted, halved, quarter = rows // parts, rows // parts // 2, rows // parts // 4
    experts = 4 * parts
    me, high = lax.axis_index("fsdp"), lax.axis_index("tp")
    z, low, x, core = me // 16, (me // 8) % 2, (me // 2) % 4, me % 2
    y = high * 2 + low
    facing = y + core * (3 - 2 * y)

    def plane(to_z, to_y):
        return to_z * 16 + (to_y % 2) * 8 + x * 2 + core, to_y // 2

    def beside(to_x, to_core):
        return me - x * 2 - core + to_x * 2 + to_core, high

    barrier = pltpu.get_barrier_semaphore()
    for step in range(1, 4):
        for there in (plane((z + step) % 4, facing), plane(z, (y + step) % 4)):
            pl.semaphore_signal(barrier, inc=1, device_id=there, device_id_type=MESH)
    for step in range(1, 8):
        pl.semaphore_signal(
            barrier, inc=1, device_id=beside((x + step // 2) % 4, (core + step) % 2), device_id_type=MESH
        )

    def loads(chunk):
        at = slice(chunk * slim, (chunk + 1) * slim)
        pieces = [
            (ref.at[:, at], fwd_ref.at[chunk, :, pl.ds(place * slim, slim)])
            for place, ref in enumerate((gate_ref, up_ref, gdir_ref, udir_ref))
        ] + [
            (ref.at[at, :], bwd_ref.at[chunk, pl.ds(place * slim, slim), :])
            for place, ref in enumerate((down_ref, ddir_ref))
        ]
        return [
            pltpu.make_async_copy(source, target, load_sem.at[chunk, place])
            for place, (source, target) in enumerate(pieces)
        ]

    row = route_ref[...].astype(jnp.float32)
    col = jnp.broadcast_to(row, (tokens, tokens)).T
    first = lax.broadcasted_iota(jnp.int32, (tokens, tokens), 0)
    second = lax.broadcasted_iota(jnp.int32, (tokens, tokens), 1)
    before = jnp.where((col == row) & (first < second), 1.0, 0.0)
    slot = row * CAPACITY + jnp.sum(before, axis=0, keepdims=True)
    key = jnp.concatenate([slot + 1024.0 * part for part in range(4)], axis=1)
    place = lax.broadcasted_iota(jnp.int32, (experts * BLOCK, 1), 0).astype(jnp.float32)
    number = jnp.floor((place + 0.5) * (1.0 / BLOCK))
    within = place - number * BLOCK
    span = jnp.floor((number + 0.5) * 0.25)
    pair = jnp.floor((number - 4.0 * span + 0.5) * 0.5)
    expert = 2.0 * number - 4.0 * span - 3.0 * pair
    part = jnp.floor((within + 0.5) * (1.0 / CAPACITY))
    wanted = expert * CAPACITY + (within - part * CAPACITY) + 1024.0 * part
    pick_ref[...] = jnp.where(wanted == key, 1.0, 0.0).astype(jnp.bfloat16)
    gate = jnp.broadcast_to(weight_ref[...], (tokens, tokens)).T[:, 0:1]
    weighted = (gate * cotan_ref[...].astype(jnp.float32)).astype(jnp.bfloat16)
    for piece in range(2):
        for side in range(2):
            lanes = slice((2 * piece + side) * fine, (2 * piece + side + 1) * fine)
            feed_ref[piece, pl.ds(side * tokens, tokens), :] = mine_ref[:, lanes]
            feed_ref[piece, pl.ds((2 + side) * tokens, tokens), :] = weighted[:, lanes]

    def gather(step, carry):
        at = pl.ds(pl.multiple_of(step * 4 * BLOCK, 4 * BLOCK), 4 * BLOCK)
        for piece in range(2):
            picked = jnp.dot(pick_ref[at, :], feed_ref[piece], preferred_element_type=jnp.float32)
            for place in range(4):
                send_ref[piece, step, place // 2, place % 2] = picked[
                    place * BLOCK : (place + 1) * BLOCK
                ].astype(jnp.bfloat16)
        return carry

    lax.fori_loop(0, parts, gather, 0)
    pl.semaphore_wait(barrier, 13)

    def transfer(here, source, target, send_sem, recv_sem, device):
        def start():
            @pl.when(here)
            def _():
                pltpu.make_async_copy(source, target, recv_sem).start()

            @pl.when(jnp.logical_not(here))
            def _():
                remote().start()

        def remote():
            return pltpu.make_async_remote_copy(
                src_ref=source, dst_ref=target, send_sem=send_sem, recv_sem=recv_sem,
                device_id=device, device_id_type=MESH,
            )

        def finish():
            @pl.when(jnp.logical_not(here))
            def _():
                remote().wait_send()

        return start, finish

    def landed(place, sem):
        pltpu.make_async_copy(place, place, sem).wait()

    def along_z(part, to_core):
        dz = part + part // 2 * (1 - 2 * (part % 2))
        to_z = (z + dz) % 4
        return transfer(
            jnp.logical_and(dz == 0, core == 0), send_ref.at[to_core, to_z], first_ref.at[part, to_core],
            z_send.at[part * 2 + to_core], z_recv.at[part * 2 + to_core], plane(to_z, facing),
        )

    def along_x(part, pair, to_core):
        to_x = pair * 2 + (high + core) % 2
        return transfer(
            jnp.logical_and(to_x == x, to_core == core),
            first_ref.at[part, to_core, pair],
            second_ref.at[part, :, pl.ds(pl.multiple_of(x * BLOCK, BLOCK), BLOCK), :],
            x_send.at[part * 4 + pair * 2 + to_core], x_recv.at[part * 4 + x], beside(to_x, to_core),
        )

    def along_y(part, to_low, to_high):
        to_y = to_high * 2 + to_low
        origin_core = (high + x) % 2
        origin = (low + origin_core * (1 - 2 * low)) * 2 + origin_core
        return transfer(
            to_y == y, second_ref.at[part, to_low], packed_ref.at[part * 4 + origin],
            y_send.at[part * 4 + to_y], y_recv.at[part * 4 + origin], plane(z, to_y),
        )

    def hop_z(part, carry):
        for to_core in range(2):
            along_z(part, to_core)[0]()
        return carry

    def hop_x(part):
        for to_core in range(2):
            landed(first_ref.at[part, to_core], z_recv.at[part * 2 + to_core])
        for pair in range(2):
            for to_core in range(2):
                along_x(part, pair, to_core)[0]()

    def hop_y(part):
        for number in range(4):
            landed(second_ref.at[part, :, pl.ds(number * BLOCK, BLOCK), :], x_recv.at[part * 4 + number])
        for to_low in range(2):
            for to_high in range(2):
                along_y(part, to_low, to_high)[0]()

    def arrive(part):
        for number in range(4):
            landed(packed_ref.at[part * 4 + number], y_recv.at[part * 4 + number])

    lax.fori_loop(0, 2, hop_z, 0)
    for chunk in range(chunks):
        for copy in loads(chunk):
            copy.start()

    sort_rows = 4 * BLOCK
    left = lax.broadcasted_iota(jnp.int32, (sort_rows, 1), 0).astype(jnp.float32)
    part = jnp.floor((left + 0.5) * (1.0 / BLOCK))
    source = jnp.floor((left - part * BLOCK + 0.5) * (1.0 / CAPACITY))
    rest = left - part * BLOCK - source * CAPACITY
    wanted = source * BLOCK + part * CAPACITY + rest
    have = lax.broadcasted_iota(jnp.int32, (1, sort_rows), 1).astype(jnp.float32)
    sorter = jnp.where(wanted == have, 1.0, 0.0).astype(jnp.bfloat16)

    def sort(group, carry):
        taken = packed_ref[group]
        ordered = jnp.dot(sorter, taken, preferred_element_type=jnp.float32).astype(jnp.bfloat16)
        to = pl.ds(pl.multiple_of(group * BLOCK, BLOCK), BLOCK)
        tok_ref[to, 0:fine] = ordered[0:BLOCK]
        tok_ref[to, fine:depth] = ordered[BLOCK : 2 * BLOCK]
        cot_ref[to, 0:fine] = ordered[2 * BLOCK : 3 * BLOCK]
        cot_ref[to, fine:depth] = ordered[3 * BLOCK : 4 * BLOCK]
        return carry


    against = (((1,), (1,)), ((), ()))

    chip = x % 2
    core_mate, chip_mate = beside(x, 1 - core), beside(x + 1 - 2 * chip, core)

    def to_core(unit):
        theirs = pl.ds(pl.multiple_of((1 - core) * halved, halved), halved)
        return pltpu.make_async_remote_copy(
            src_ref=part_ref.at[unit % 4, theirs, :], dst_ref=core_in.at[unit],
            send_sem=core_send.at[unit], recv_sem=core_recv.at[unit],
            device_id=core_mate, device_id_type=MESH,
        )

    def to_chip(unit):
        return pltpu.make_async_remote_copy(
            src_ref=chip_out.at[unit], dst_ref=chip_in.at[unit],
            send_sem=chip_send.at[unit], recv_sem=chip_recv.at[unit],
            device_id=chip_mate, device_id_type=MESH,
        )

    def back(unit, where):
        begin = unit // chunks * parted + core * halved + where * quarter
        place = curved_ref.at[unit % chunks, pl.ds(pl.multiple_of(begin, quarter), quarter), :]
        return pltpu.make_async_remote_copy(
            src_ref=place, dst_ref=place,
            send_sem=back_send.at[unit], recv_sem=back_recv.at[unit],
            device_id=chip_mate, device_id_type=MESH,
        )

    def last(unit, where):
        begin = unit // chunks * parted + where * halved
        place = curved_ref.at[unit % chunks, pl.ds(pl.multiple_of(begin, halved), halved), :]
        return pltpu.make_async_remote_copy(
            src_ref=place, dst_ref=place,
            send_sem=last_send.at[unit], recv_sem=last_recv.at[unit],
            device_id=core_mate, device_id_type=MESH,
        )

    def products(unit):
        @pl.when(unit < chunks)
        def _():
            for place in range(6):
                loaded = (
                    bwd_ref.at[unit, pl.ds(0, slim), :] if place >= 4 else fwd_ref.at[unit, :, pl.ds(0, slim)]
                )
                pltpu.make_async_copy(loaded, loaded, load_sem.at[unit, place]).wait()

        @pl.when(unit >= 4)
        def _():
            to_core(unit - 4).wait_send()

        chunk = unit % chunks
        at = pl.ds(pl.multiple_of(unit // chunks * parted, parted), parted)
        part_ref[unit % 4, :, 0 : 4 * slim] = jnp.dot(
            tok_ref[at, :], fwd_ref[chunk], preferred_element_type=jnp.float32
        )
        part_ref[unit % 4, :, 4 * slim : 6 * slim] = lax.dot_general(
            cot_ref[at, :], bwd_ref[chunk], against, preferred_element_type=jnp.float32
        )
        to_core(unit).start()

    def core_sum(unit):
        to_core(unit).wait_recv()
        slot = unit % 4

        def whole(where):
            own = pl.ds(pl.multiple_of(core * halved + where * quarter, quarter), quarter)
            return part_ref[slot, own, :] + core_in[unit, pl.ds(pl.multiple_of(where * quarter, quarter), quarter), :]

        chip_out[unit] = whole(1 - chip).astype(jnp.bfloat16)
        to_chip(unit).start()
        chip_keep[unit] = whole(chip)

    def partial_products(part):
        lax.fori_loop(part * 4, part * 4 + 4, sort, 0)

        def both(step, carry):
            @pl.when(step < chunks)
            def _():
                products(part * chunks + step)

            @pl.when(step > 0)
            def _():
                core_sum(part * chunks + step - 1)

            return carry

        lax.fori_loop(0, chunks + 1, both, 0)

    def curve(unit, carry):
        to_chip(unit).wait_recv()
        total = chip_keep[unit] + chip_in[unit].astype(jnp.float32)
        begin = unit // chunks * parted + core * halved + chip * quarter
        curved_ref[unit % chunks, pl.ds(pl.multiple_of(begin, quarter), quarter), :] = curvature(total, slim)
        back(unit, chip).start()
        return carry

    def cross(step, carry):
        hop_x(step)

        @pl.when(step + 2 < parts)
        def _():
            hop_z(step + 2, 0)

        @pl.when(step == 1)
        def _():
            hop_y(0)

        return carry

    lax.fori_loop(0, parts, cross, 0)

    rows_out = [
        pltpu.make_async_copy(flip_ref, flip_out, out_sem.at[units]),
        pltpu.make_async_copy(cot_ref, cot_out, out_sem.at[units + 1]),
    ]

    def curved_copy(unit):
        at = pl.ds(pl.multiple_of(unit // chunks * parted, parted), parted)
        chunk = unit % chunks
        return pltpu.make_async_copy(curved_ref.at[chunk, at, :], curved_out.at[chunk, at, :], out_sem.at[unit])

    def advance(step, carry):
        @pl.when(step < parts)
        def _():
            arrive(step)

        @pl.when(step + 1 < parts)
        def _():
            hop_y(step + 1)

        @pl.when(step == parts)
        def _():
            flip_ref[...] = tok_ref[...].T
            for copy in rows_out:
                copy.start()

        @pl.when(step >= 2)
        def _():
            lax.fori_loop((step - 2) * chunks, (step - 2) * chunks + chunks, curve, 0)

        @pl.when(step < parts)
        def _():
            partial_products(step)

        return carry

    lax.fori_loop(0, parts + 2, advance, 0)
    def spread(unit, carry):
        back(unit, 1 - chip).wait_recv()
        last(unit, core).start()
        return carry

    lax.fori_loop(0, units, spread, 0)

    def finish(unit, carry):
        last(unit, 1 - core).wait_recv()
        back(unit, chip).wait_send()
        last(unit, core).wait_send()
        curved_copy(unit).start()

        @pl.when(unit >= units - 4)
        def _():
            to_core(unit).wait_send()

        to_chip(unit).wait_send()
        return carry

    lax.fori_loop(0, units, finish, 0)
    def sent(part, carry):
        for first in range(2):
            along_z(part, first)[1]()
            for second in range(2):
                along_x(part, first, second)[1]()
                along_y(part, first, second)[1]()
        return carry

    lax.fori_loop(0, parts, sent, 0)

    def written(unit, carry):
        curved_copy(unit).wait()
        return carry

    lax.fori_loop(0, units, written, 0)
    for copy in rows_out:
        copy.wait()


def curvature(total, width):
    gate_pre, up_pre, gate_tan, up_tan, grad_hidden, tan_grad = (
        total[:, width * place : width * (place + 1)] for place in range(6)
    )
    sigmoid_gate = jax.nn.sigmoid(gate_pre)
    silu_gate = gate_pre * sigmoid_gate
    slope = sigmoid_gate * (1.0 + gate_pre * (1.0 - sigmoid_gate))
    bend = sigmoid_gate * (1.0 - sigmoid_gate) * (2.0 + gate_pre * (1.0 - 2.0 * sigmoid_gate))
    tan_gate = (
        tan_grad * up_pre * slope
        + grad_hidden * up_tan * slope
        + grad_hidden * up_pre * bend * gate_tan
    )
    tan_up = tan_grad * silu_gate + grad_hidden * slope * gate_tan
    tan_hidden = slope * gate_tan * up_pre + silu_gate * up_tan
    return jnp.concatenate([tan_gate, tan_up, tan_hidden], axis=1).astype(jnp.bfloat16)


def product_kernel(
    flip_in, cot_in, curved_in, gate_out, up_out, down_out,
    flip_ref, cot_ref, curved_ref, gate_ref, up_ref, down_ref, load_sem, store_sem,
):
    chunks, _, wide = curved_ref.shape
    slim = wide // 3
    half = flip_ref.shape[0] // 2
    sides = [pl.ds(0, half), pl.ds(half, half)]
    curved_in_copy = [
        pltpu.make_async_copy(curved_in.at[chunk], curved_ref.at[chunk], load_sem.at[chunk])
        for chunk in range(chunks)
    ]
    flip_copy = [
        pltpu.make_async_copy(flip_in.at[side], flip_ref.at[side], load_sem.at[chunks + place])
        for place, side in enumerate(sides)
    ]
    cot_copy = pltpu.make_async_copy(cot_in, cot_ref, load_sem.at[chunks + 2])
    for copy in [curved_in_copy[0], *flip_copy, *curved_in_copy[1:], cot_copy]:
        copy.start()
    stores = []

    def store(source, target):
        copy = pltpu.make_async_copy(source, target, store_sem.at[len(stores)])
        copy.start()
        stores.append(copy)

    for chunk in range(chunks):
        curved_in_copy[chunk].wait()
        lanes = pl.ds(chunk * slim, slim)
        for place, side in enumerate(sides):
            if chunk == 0:
                flip_copy[place].wait()
            both = jnp.dot(
                flip_ref[side, :], curved_ref[chunk, :, 0 : 2 * slim], preferred_element_type=jnp.float32
            )
            gate_ref[side, lanes] = both[:, 0:slim]
            up_ref[side, lanes] = both[:, slim : 2 * slim]
            store(gate_ref.at[side, lanes], gate_out.at[side, lanes])
            store(up_ref.at[side, lanes], up_out.at[side, lanes])
    cot_copy.wait()
    for chunk in range(chunks):
        lanes = pl.ds(chunk * slim, slim)
        down_ref[lanes, :] = lax.dot_general(
            curved_ref[chunk, :, 2 * slim : 3 * slim],
            cot_ref[...],
            (((0,), (0,)), ((), ())),
            preferred_element_type=jnp.float32,
        )
        store(down_ref.at[lanes, :], down_out.at[lanes, :])
    for copy in stores:
        copy.wait()


def local(
    tokens, cotangent, routes, gates, gate_proj, up_proj, down_proj, gate_dir, up_dir, down_dir
):
    count, width = tokens.shape
    groups = lax.axis_size("fsdp")
    experts = groups // 4
    depth, hidden = gate_proj.shape[1:]
    rows = groups * CAPACITY
    slim = 256
    chunks = hidden // slim
    bf16, f32 = jnp.bfloat16, jnp.float32

    parts = 4
    units = parts * chunks
    parted = rows // parts
    flipped, cot, curved = pl.pallas_call(
        layer_kernel,
        name="layer",
        out_shape=(
            jax.ShapeDtypeStruct((depth, rows), bf16),
            jax.ShapeDtypeStruct((rows, depth), bf16),
            jax.ShapeDtypeStruct((chunks, rows, 3 * slim), bf16),
        ),
        in_specs=[SPACE] * 4 + [HBM] * 6,
        out_specs=(HBM,) * 3,
        scratch_shapes=[
            pltpu.VMEM((depth, rows), bf16),
            pltpu.VMEM((rows, depth), bf16),
            pltpu.VMEM((chunks, rows, 3 * slim), bf16),
            pltpu.VMEM((2, 4, 2, 2, BLOCK, width // 4), bf16),
            pltpu.VMEM((experts * BLOCK, 4 * count), bf16),
            pltpu.VMEM((2, 4 * count, width // 4), bf16),
            pltpu.VMEM((parts, 2, 2, 2, BLOCK, width // 4), bf16),
            pltpu.VMEM((parts, 2, 4 * BLOCK, width // 4), bf16),
            pltpu.VMEM((parts * 4, 4 * BLOCK, width // 4), bf16),
            pltpu.VMEM((rows, depth), bf16),
            pltpu.VMEM((chunks, depth, 4 * slim), bf16),
            pltpu.VMEM((chunks, 2 * slim, depth), bf16),
            pltpu.VMEM((4, parted, 6 * slim), f32),
            pltpu.VMEM((units, parted // 2, 6 * slim), f32),
            pltpu.VMEM((units, parted // 4, 6 * slim), f32),
            pltpu.VMEM((units, parted // 4, 6 * slim), bf16),
            pltpu.VMEM((units, parted // 4, 6 * slim), bf16),
        ]
        + [pltpu.SemaphoreType.DMA((parts * 2,))] * 2
        + [pltpu.SemaphoreType.DMA((parts * 4,))] * 4
        + [pltpu.SemaphoreType.DMA((chunks, 6))]
        + [pltpu.SemaphoreType.DMA((units,))] * 8
        + [pltpu.SemaphoreType.DMA((units + 2,))],
        compiler_params=pltpu.CompilerParams(
            collective_id=0, has_side_effects=True, vmem_limit_bytes=VMEM_LIMIT
        ),
    )(
        tokens, cotangent, routes.reshape(1, count), gates.reshape(1, count),
        gate_proj[0], up_proj[0], gate_dir[0], up_dir[0], down_proj[0], down_dir[0],
    )

    hess_gate, hess_up, hess_down = pl.pallas_call(
        product_kernel,
        name="products",
        out_shape=(
            jax.ShapeDtypeStruct((depth, hidden), f32),
            jax.ShapeDtypeStruct((depth, hidden), f32),
            jax.ShapeDtypeStruct((hidden, depth), f32),
        ),
        in_specs=[HBM] * 3,
        out_specs=(HBM,) * 3,
        scratch_shapes=[
            pltpu.VMEM((depth, rows), bf16),
            pltpu.VMEM((rows, depth), bf16),
            pltpu.VMEM((chunks, rows, 3 * slim), bf16),
            pltpu.VMEM((depth, hidden), f32),
            pltpu.VMEM((depth, hidden), f32),
            pltpu.VMEM((hidden, depth), f32),
            pltpu.SemaphoreType.DMA((chunks + 3,)),
            pltpu.SemaphoreType.DMA((5 * chunks,)),
        ],
        compiler_params=pltpu.CompilerParams(vmem_limit_bytes=VMEM_LIMIT),
    )(flipped, cot, curved)
    return (hess_gate[None], hess_up[None], hess_down[None])


def solution(mesh):
    return jax.shard_map(
        local,
        mesh=mesh,
        in_specs=(
            P("fsdp", "tp"),
            P("fsdp", "tp"),
            P("fsdp", None),
            P("fsdp", None),
            P("fsdp", None, "tp"),
            P("fsdp", None, "tp"),
            P("fsdp", "tp", None),
            P("fsdp", None, "tp"),
            P("fsdp", None, "tp"),
            P("fsdp", "tp", None),
        ),
        out_specs=(P("fsdp", None, "tp"), P("fsdp", None, "tp"), P("fsdp", "tp", None)),
        check_vma=False,
    )
```

```python
import jax
import jax.numpy as jnp
from jax import lax
from jax.experimental import pallas as pl
from jax.experimental.pallas import tpu as pltpu
from jax.sharding import PartitionSpec as P

MESH = pl.DeviceIdType.MESH
CAPACITY = 12
BLOCK = 4 * CAPACITY
VMEM_LIMIT = 60 * 1024 * 1024
SPACE = pl.BlockSpec(memory_space=pltpu.VMEM)
HBM = pl.BlockSpec(memory_space=pl.ANY)


def layer_kernel(
    mine_ref, cotan_ref, route_ref, weight_ref, gate_ref, up_ref, gdir_ref, udir_ref, down_ref, ddir_ref,
    flip_out, cot_out, curved_out,
    flip_ref, cot_ref, curved_ref, send_ref, pick_ref, feed_ref, early_ref, first_ref, second_ref, packed_ref, tok_ref,
    fwd_ref, bwd_ref, part_ref, core_in, chip_keep, chip_out, chip_in,
    z_send, z_recv, x_send, x_recv, y_send, y_recv, early_y_send, early_y_recv, early_x_send, early_x_recv,
    load_sem, core_send, core_recv, chip_send, chip_recv, back_send, back_recv, last_send, last_recv, out_sem,
):
    tokens, width = mine_ref.shape
    fine = width // 4
    rows, depth = tok_ref.shape
    chunks, _, wide = curved_ref.shape
    slim = wide // 3
    parts = packed_ref.shape[0] // 4
    units = parts * chunks
    parted, halved, quarter = rows // parts, rows // parts // 2, rows // parts // 4
    experts = 4 * parts
    me, high = lax.axis_index("fsdp"), lax.axis_index("tp")
    z, low, x, core = me // 16, (me // 8) % 2, (me // 2) % 4, me % 2
    y = high * 2 + low
    facing = y + core * (3 - 2 * y)

    def plane(to_z, to_y):
        return to_z * 16 + (to_y % 2) * 8 + x * 2 + core, to_y // 2

    def beside(to_x, to_core):
        return me - x * 2 - core + to_x * 2 + to_core, high

    barrier = pltpu.get_barrier_semaphore()
    for step in range(1, 4):
        for there in (plane((z + step) % 4, facing), plane(z, (y + step) % 4)):
            pl.semaphore_signal(barrier, inc=1, device_id=there, device_id_type=MESH)
    for step in range(1, 8):
        pl.semaphore_signal(
            barrier, inc=1, device_id=beside((x + step // 2) % 4, (core + step) % 2), device_id_type=MESH
        )

    def loads(chunk):
        at = slice(chunk * slim, (chunk + 1) * slim)
        pieces = [
            (ref.at[:, at], fwd_ref.at[chunk, :, pl.ds(place * slim, slim)])
            for place, ref in enumerate((gate_ref, up_ref, gdir_ref, udir_ref))
        ] + [
            (ref.at[at, :], bwd_ref.at[chunk, pl.ds(place * slim, slim), :])
            for place, ref in enumerate((down_ref, ddir_ref))
        ]
        return [
            pltpu.make_async_copy(source, target, load_sem.at[chunk, place])
            for place, (source, target) in enumerate(pieces)
        ]

    row = route_ref[...].astype(jnp.float32)
    col = jnp.broadcast_to(row, (tokens, tokens)).T
    first = lax.broadcasted_iota(jnp.int32, (tokens, tokens), 0)
    second = lax.broadcasted_iota(jnp.int32, (tokens, tokens), 1)
    before = jnp.where((col == row) & (first < second), 1.0, 0.0)
    slot = row * CAPACITY + jnp.sum(before, axis=0, keepdims=True)
    key = jnp.concatenate([slot + 1024.0 * part for part in range(4)], axis=1)
    place = lax.broadcasted_iota(jnp.int32, (experts * BLOCK, 1), 0).astype(jnp.float32)
    number = jnp.floor((place + 0.5) * (1.0 / BLOCK))
    within = place - number * BLOCK
    span = jnp.floor((number + 0.5) * 0.25)
    pair = jnp.floor((number - 4.0 * span + 0.5) * 0.5)
    expert = 2.0 * number - 4.0 * span - 3.0 * pair
    part = jnp.floor((within + 0.5) * (1.0 / CAPACITY))
    wanted = expert * CAPACITY + (within - part * CAPACITY) + 1024.0 * part
    pick_ref[...] = jnp.where(wanted == key, 1.0, 0.0).astype(jnp.bfloat16)
    gate = jnp.broadcast_to(weight_ref[...], (tokens, tokens)).T[:, 0:1]
    weighted = (gate * cotan_ref[...].astype(jnp.float32)).astype(jnp.bfloat16)
    for piece in range(2):
        for side in range(2):
            lanes = slice((2 * piece + side) * fine, (2 * piece + side + 1) * fine)
            feed_ref[piece, pl.ds(side * tokens, tokens), :] = mine_ref[:, lanes]
            feed_ref[piece, pl.ds((2 + side) * tokens, tokens), :] = weighted[:, lanes]

    def gather(step, carry):
        at = pl.ds(pl.multiple_of(step * 4 * BLOCK, 4 * BLOCK), 4 * BLOCK)
        for piece in range(2):
            picked = jnp.dot(pick_ref[at, :], feed_ref[piece], preferred_element_type=jnp.float32)
            for place in range(4):
                send_ref[piece, step, place // 2, place % 2] = picked[
                    place * BLOCK : (place + 1) * BLOCK
                ].astype(jnp.bfloat16)
        return carry

    lax.fori_loop(0, parts, gather, 0)
    pl.semaphore_wait(barrier, 13)

    def transfer(here, source, target, send_sem, recv_sem, device):
        def start():
            @pl.when(here)
            def _():
                pltpu.make_async_copy(source, target, recv_sem).start()

            @pl.when(jnp.logical_not(here))
            def _():
                remote().start()

        def remote():
            return pltpu.make_async_remote_copy(
                src_ref=source, dst_ref=target, send_sem=send_sem, recv_sem=recv_sem,
                device_id=device, device_id_type=MESH,
            )

        def finish():
            @pl.when(jnp.logical_not(here))
            def _():
                remote().wait_send()

        return start, finish

    def landed(place, sem):
        pltpu.make_async_copy(place, place, sem).wait()

    def along_z(part, to_core):
        dz = part + part // 2 * (1 - 2 * (part % 2))
        to_z = (z + dz) % 4
        return transfer(
            jnp.logical_and(dz == 0, core == 0), send_ref.at[to_core, to_z], first_ref.at[part, to_core],
            z_send.at[part * 2 + to_core], z_recv.at[part * 2 + to_core], plane(to_z, facing),
        )

    def along_x(part, pair, to_core):
        to_x = pair * 2 + (high + core) % 2
        return transfer(
            jnp.logical_and(to_x == x, to_core == core),
            first_ref.at[part, to_core, pair],
            second_ref.at[part, :, pl.ds(pl.multiple_of(x * BLOCK, BLOCK), BLOCK), :],
            x_send.at[part * 4 + pair * 2 + to_core], x_recv.at[part * 4 + x], beside(to_x, to_core),
        )

    def along_y(part, to_low, to_high):
        to_y = to_high * 2 + to_low
        origin_core = (high + x) % 2
        origin = (low + origin_core * (1 - 2 * low)) * 2 + origin_core
        return transfer(
            to_y == y, second_ref.at[part, to_low], packed_ref.at[part * 4 + origin],
            y_send.at[part * 4 + to_y], y_recv.at[part * 4 + origin], plane(z, to_y),
        )

    def early_y(to_low, to_high):
        to_y = to_high * 2 + to_low
        return transfer(
            to_y == y, send_ref.at[:, z, :, to_low], early_ref.at[y],
            early_y_send.at[to_y], early_y_recv.at[y], plane(z, to_y),
        )

    def early_x(turn, pair, to_core):
        from_y = (y + turn) % 4
        origin = (from_y % 2) * 2 + core
        to_x = pair * 2 + from_y // 2
        return transfer(
            jnp.logical_and(to_x == x, to_core == core),
            early_ref.at[from_y, to_core, pair],
            packed_ref.at[origin, pl.ds(pl.multiple_of(x * BLOCK, BLOCK), BLOCK), :],
            early_x_send.at[turn * 4 + pair * 2 + to_core], early_x_recv.at[origin * 4 + x], beside(to_x, to_core),
        )

    def hop_early():
        for to_low in range(2):
            for to_high in range(2):
                early_y(to_low, to_high)[0]()

    def pass_early():
        for turn in (0, 1, 3, 2):
            from_y = (y + turn) % 4
            landed(early_ref.at[from_y], early_y_recv.at[from_y])
            for pair in range(2):
                for to_core in range(2):
                    early_x(turn, pair, to_core)[0]()

    def arrive_early():
        for origin in range(4):
            for number in range(4):
                landed(
                    packed_ref.at[origin, pl.ds(number * BLOCK, BLOCK), :], early_x_recv.at[origin * 4 + number]
                )

    def hop_z(part, carry):
        for to_core in range(2):
            along_z(part, to_core)[0]()
        return carry

    def hop_x(part):
        for to_core in range(2):
            landed(first_ref.at[part, to_core], z_recv.at[part * 2 + to_core])
        for pair in range(2):
            for to_core in range(2):
                along_x(part, pair, to_core)[0]()

    def hop_y(part):
        for number in range(4):
            landed(second_ref.at[part, :, pl.ds(number * BLOCK, BLOCK), :], x_recv.at[part * 4 + number])
        for to_low in range(2):
            for to_high in range(2):
                along_y(part, to_low, to_high)[0]()

    def arrive(part):
        for number in range(4):
            landed(packed_ref.at[part * 4 + number], y_recv.at[part * 4 + number])

    hop_early()
    hop_z(1, 0)
    hop_z(2, 0)
    for chunk in range(chunks):
        for copy in loads(chunk):
            copy.start()

    sort_rows = 4 * BLOCK
    left = lax.broadcasted_iota(jnp.int32, (sort_rows, 1), 0).astype(jnp.float32)
    part = jnp.floor((left + 0.5) * (1.0 / BLOCK))
    source = jnp.floor((left - part * BLOCK + 0.5) * (1.0 / CAPACITY))
    rest = left - part * BLOCK - source * CAPACITY
    wanted = source * BLOCK + part * CAPACITY + rest
    have = lax.broadcasted_iota(jnp.int32, (1, sort_rows), 1).astype(jnp.float32)
    sorter = jnp.where(wanted == have, 1.0, 0.0).astype(jnp.bfloat16)

    def sort(group, carry):
        taken = packed_ref[group]
        ordered = jnp.dot(sorter, taken, preferred_element_type=jnp.float32).astype(jnp.bfloat16)
        to = pl.ds(pl.multiple_of(group * BLOCK, BLOCK), BLOCK)
        tok_ref[to, 0:fine] = ordered[0:BLOCK]
        tok_ref[to, fine:depth] = ordered[BLOCK : 2 * BLOCK]
        cot_ref[to, 0:fine] = ordered[2 * BLOCK : 3 * BLOCK]
        cot_ref[to, fine:depth] = ordered[3 * BLOCK : 4 * BLOCK]
        return carry


    against = (((1,), (1,)), ((), ()))

    chip = x % 2
    core_mate, chip_mate = beside(x, 1 - core), beside(x + 1 - 2 * chip, core)

    def to_core(unit):
        theirs = pl.ds(pl.multiple_of((1 - core) * halved, halved), halved)
        return pltpu.make_async_remote_copy(
            src_ref=part_ref.at[unit % 4, theirs, :], dst_ref=core_in.at[unit],
            send_sem=core_send.at[unit], recv_sem=core_recv.at[unit],
            device_id=core_mate, device_id_type=MESH,
        )

    def to_chip(unit):
        return pltpu.make_async_remote_copy(
            src_ref=chip_out.at[unit], dst_ref=chip_in.at[unit],
            send_sem=chip_send.at[unit], recv_sem=chip_recv.at[unit],
            device_id=chip_mate, device_id_type=MESH,
        )

    def back(unit, where):
        begin = unit // chunks * parted + core * halved + where * quarter
        place = curved_ref.at[unit % chunks, pl.ds(pl.multiple_of(begin, quarter), quarter), :]
        return pltpu.make_async_remote_copy(
            src_ref=place, dst_ref=place,
            send_sem=back_send.at[unit], recv_sem=back_recv.at[unit],
            device_id=chip_mate, device_id_type=MESH,
        )

    def last(unit, where):
        begin = unit // chunks * parted + where * halved
        place = curved_ref.at[unit % chunks, pl.ds(pl.multiple_of(begin, halved), halved), :]
        return pltpu.make_async_remote_copy(
            src_ref=place, dst_ref=place,
            send_sem=last_send.at[unit], recv_sem=last_recv.at[unit],
            device_id=core_mate, device_id_type=MESH,
        )

    def products(unit):
        @pl.when(unit < chunks)
        def _():
            for place in range(6):
                loaded = (
                    bwd_ref.at[unit, pl.ds(0, slim), :] if place >= 4 else fwd_ref.at[unit, :, pl.ds(0, slim)]
                )
                pltpu.make_async_copy(loaded, loaded, load_sem.at[unit, place]).wait()

        @pl.when(unit >= 4)
        def _():
            to_core(unit - 4).wait_send()

        chunk = unit % chunks
        at = pl.ds(pl.multiple_of(unit // chunks * parted, parted), parted)
        part_ref[unit % 4, :, 0 : 4 * slim] = jnp.dot(
            tok_ref[at, :], fwd_ref[chunk], preferred_element_type=jnp.float32
        )
        part_ref[unit % 4, :, 4 * slim : 6 * slim] = lax.dot_general(
            cot_ref[at, :], bwd_ref[chunk], against, preferred_element_type=jnp.float32
        )
        to_core(unit).start()

    def core_sum(unit):
        to_core(unit).wait_recv()
        slot = unit % 4

        def whole(where):
            own = pl.ds(pl.multiple_of(core * halved + where * quarter, quarter), quarter)
            return part_ref[slot, own, :] + core_in[unit, pl.ds(pl.multiple_of(where * quarter, quarter), quarter), :]

        chip_out[unit] = whole(1 - chip).astype(jnp.bfloat16)
        to_chip(unit).start()
        chip_keep[unit] = whole(chip)

    def partial_products(part):
        lax.fori_loop(part * 4, part * 4 + 4, sort, 0)

        def both(step, carry):
            @pl.when(step < chunks)
            def _():
                products(part * chunks + step)

            @pl.when(step > 0)
            def _():
                core_sum(part * chunks + step - 1)

            return carry

        lax.fori_loop(0, chunks + 1, both, 0)

    def curve(unit, carry):
        to_chip(unit).wait_recv()
        total = chip_keep[unit] + chip_in[unit].astype(jnp.float32)
        begin = unit // chunks * parted + core * halved + chip * quarter
        curved_ref[unit % chunks, pl.ds(pl.multiple_of(begin, quarter), quarter), :] = curvature(total, slim)
        back(unit, chip).start()
        return carry

    pass_early()
    hop_z(3, 0)
    hop_x(1)
    hop_x(2)
    hop_x(3)

    rows_out = [
        pltpu.make_async_copy(flip_ref, flip_out, out_sem.at[units]),
        pltpu.make_async_copy(cot_ref, cot_out, out_sem.at[units + 1]),
    ]

    def curved_copy(unit):
        at = pl.ds(pl.multiple_of(unit // chunks * parted, parted), parted)
        chunk = unit % chunks
        return pltpu.make_async_copy(curved_ref.at[chunk, at, :], curved_out.at[chunk, at, :], out_sem.at[unit])

    def advance(step, carry):
        @pl.when(step == 0)
        def _():
            arrive_early()
            hop_y(1)

        @pl.when(jnp.logical_and(step >= 1, step < parts))
        def _():
            arrive(step)

        @pl.when(jnp.logical_and(step >= 1, step + 1 < parts))
        def _():
            hop_y(step + 1)

        @pl.when(step == parts)
        def _():
            flip_ref[...] = tok_ref[...].T
            for copy in rows_out:
                copy.start()

        @pl.when(step >= 2)
        def _():
            lax.fori_loop((step - 2) * chunks, (step - 2) * chunks + chunks, curve, 0)

        @pl.when(step < parts)
        def _():
            partial_products(step)

        return carry

    lax.fori_loop(0, parts + 2, advance, 0)
    def spread(unit, carry):
        back(unit, 1 - chip).wait_recv()
        last(unit, core).start()
        return carry

    lax.fori_loop(0, units, spread, 0)

    def finish(unit, carry):
        last(unit, 1 - core).wait_recv()
        back(unit, chip).wait_send()
        last(unit, core).wait_send()
        curved_copy(unit).start()

        @pl.when(unit >= units - 4)
        def _():
            to_core(unit).wait_send()

        to_chip(unit).wait_send()
        return carry

    lax.fori_loop(0, units, finish, 0)
    def sent(part, carry):
        for first in range(2):
            along_z(part, first)[1]()
            for second in range(2):
                along_x(part, first, second)[1]()
                along_y(part, first, second)[1]()
        return carry

    lax.fori_loop(1, parts, sent, 0)
    for first in range(2):
        for second in range(2):
            early_y(first, second)[1]()
            for turn in range(4):
                early_x(turn, first, second)[1]()

    def written(unit, carry):
        curved_copy(unit).wait()
        return carry

    lax.fori_loop(0, units, written, 0)
    for copy in rows_out:
        copy.wait()


def curvature(total, width):
    gate_pre, up_pre, gate_tan, up_tan, grad_hidden, tan_grad = (
        total[:, width * place : width * (place + 1)] for place in range(6)
    )
    sigmoid_gate = jax.nn.sigmoid(gate_pre)
    silu_gate = gate_pre * sigmoid_gate
    slope = sigmoid_gate * (1.0 + gate_pre * (1.0 - sigmoid_gate))
    bend = sigmoid_gate * (1.0 - sigmoid_gate) * (2.0 + gate_pre * (1.0 - 2.0 * sigmoid_gate))
    tan_gate = (
        tan_grad * up_pre * slope
        + grad_hidden * up_tan * slope
        + grad_hidden * up_pre * bend * gate_tan
    )
    tan_up = tan_grad * silu_gate + grad_hidden * slope * gate_tan
    tan_hidden = slope * gate_tan * up_pre + silu_gate * up_tan
    return jnp.concatenate([tan_gate, tan_up, tan_hidden], axis=1).astype(jnp.bfloat16)


def product_kernel(
    flip_in, cot_in, curved_in, gate_out, up_out, down_out,
    flip_ref, cot_ref, curved_ref, gate_ref, up_ref, down_ref, load_sem, store_sem,
):
    chunks, _, wide = curved_ref.shape
    slim = wide // 3
    half = flip_ref.shape[0] // 2
    sides = [pl.ds(0, half), pl.ds(half, half)]
    curved_in_copy = [
        pltpu.make_async_copy(curved_in.at[chunk], curved_ref.at[chunk], load_sem.at[chunk])
        for chunk in range(chunks)
    ]
    flip_copy = [
        pltpu.make_async_copy(flip_in.at[side], flip_ref.at[side], load_sem.at[chunks + place])
        for place, side in enumerate(sides)
    ]
    cot_copy = pltpu.make_async_copy(cot_in, cot_ref, load_sem.at[chunks + 2])
    for copy in [curved_in_copy[0], *flip_copy, *curved_in_copy[1:], cot_copy]:
        copy.start()
    stores = []

    def store(source, target):
        copy = pltpu.make_async_copy(source, target, store_sem.at[len(stores)])
        copy.start()
        stores.append(copy)

    for chunk in range(chunks):
        curved_in_copy[chunk].wait()
        lanes = pl.ds(chunk * slim, slim)
        for place, side in enumerate(sides):
            if chunk == 0:
                flip_copy[place].wait()
            both = jnp.dot(
                flip_ref[side, :], curved_ref[chunk, :, 0 : 2 * slim], preferred_element_type=jnp.float32
            )
            gate_ref[side, lanes] = both[:, 0:slim]
            up_ref[side, lanes] = both[:, slim : 2 * slim]
            store(gate_ref.at[side, lanes], gate_out.at[side, lanes])
            store(up_ref.at[side, lanes], up_out.at[side, lanes])
    cot_copy.wait()
    for chunk in range(chunks):
        lanes = pl.ds(chunk * slim, slim)
        down_ref[lanes, :] = lax.dot_general(
            curved_ref[chunk, :, 2 * slim : 3 * slim],
            cot_ref[...],
            (((0,), (0,)), ((), ())),
            preferred_element_type=jnp.float32,
        )
        store(down_ref.at[lanes, :], down_out.at[lanes, :])
    for copy in stores:
        copy.wait()


def local(
    tokens, cotangent, routes, gates, gate_proj, up_proj, down_proj, gate_dir, up_dir, down_dir
):
    count, width = tokens.shape
    groups = lax.axis_size("fsdp")
    experts = groups // 4
    depth, hidden = gate_proj.shape[1:]
    rows = groups * CAPACITY
    slim = 256
    chunks = hidden // slim
    bf16, f32 = jnp.bfloat16, jnp.float32

    parts = 4
    units = parts * chunks
    parted = rows // parts
    flipped, cot, curved = pl.pallas_call(
        layer_kernel,
        name="layer",
        out_shape=(
            jax.ShapeDtypeStruct((depth, rows), bf16),
            jax.ShapeDtypeStruct((rows, depth), bf16),
            jax.ShapeDtypeStruct((chunks, rows, 3 * slim), bf16),
        ),
        in_specs=[SPACE] * 4 + [HBM] * 6,
        out_specs=(HBM,) * 3,
        scratch_shapes=[
            pltpu.VMEM((depth, rows), bf16),
            pltpu.VMEM((rows, depth), bf16),
            pltpu.VMEM((chunks, rows, 3 * slim), bf16),
            pltpu.VMEM((2, 4, 2, 2, BLOCK, width // 4), bf16),
            pltpu.VMEM((experts * BLOCK, 4 * count), bf16),
            pltpu.VMEM((2, 4 * count, width // 4), bf16),
            pltpu.VMEM((4, 2, 2, BLOCK, width // 4), bf16),
            pltpu.VMEM((parts, 2, 2, 2, BLOCK, width // 4), bf16),
            pltpu.VMEM((parts, 2, 4 * BLOCK, width // 4), bf16),
            pltpu.VMEM((parts * 4, 4 * BLOCK, width // 4), bf16),
            pltpu.VMEM((rows, depth), bf16),
            pltpu.VMEM((chunks, depth, 4 * slim), bf16),
            pltpu.VMEM((chunks, 2 * slim, depth), bf16),
            pltpu.VMEM((4, parted, 6 * slim), f32),
            pltpu.VMEM((units, parted // 2, 6 * slim), f32),
            pltpu.VMEM((units, parted // 4, 6 * slim), f32),
            pltpu.VMEM((units, parted // 4, 6 * slim), bf16),
            pltpu.VMEM((units, parted // 4, 6 * slim), bf16),
        ]
        + [pltpu.SemaphoreType.DMA((parts * 2,))] * 2
        + [pltpu.SemaphoreType.DMA((parts * 4,))] * 4
        + [pltpu.SemaphoreType.DMA((4,))] * 2
        + [pltpu.SemaphoreType.DMA((16,))] * 2
        + [pltpu.SemaphoreType.DMA((chunks, 6))]
        + [pltpu.SemaphoreType.DMA((units,))] * 8
        + [pltpu.SemaphoreType.DMA((units + 2,))],
        compiler_params=pltpu.CompilerParams(
            collective_id=0, has_side_effects=True, vmem_limit_bytes=VMEM_LIMIT
        ),
    )(
        tokens, cotangent, routes.reshape(1, count), gates.reshape(1, count),
        gate_proj[0], up_proj[0], gate_dir[0], up_dir[0], down_proj[0], down_dir[0],
    )

    hess_gate, hess_up, hess_down = pl.pallas_call(
        product_kernel,
        name="products",
        out_shape=(
            jax.ShapeDtypeStruct((depth, hidden), f32),
            jax.ShapeDtypeStruct((depth, hidden), f32),
            jax.ShapeDtypeStruct((hidden, depth), f32),
        ),
        in_specs=[HBM] * 3,
        out_specs=(HBM,) * 3,
        scratch_shapes=[
            pltpu.VMEM((depth, rows), bf16),
            pltpu.VMEM((rows, depth), bf16),
            pltpu.VMEM((chunks, rows, 3 * slim), bf16),
            pltpu.VMEM((depth, hidden), f32),
            pltpu.VMEM((depth, hidden), f32),
            pltpu.VMEM((hidden, depth), f32),
            pltpu.SemaphoreType.DMA((chunks + 3,)),
            pltpu.SemaphoreType.DMA((5 * chunks,)),
        ],
        compiler_params=pltpu.CompilerParams(vmem_limit_bytes=VMEM_LIMIT),
    )(flipped, cot, curved)
    return (hess_gate[None], hess_up[None], hess_down[None])


def solution(mesh):
    return jax.shard_map(
        local,
        mesh=mesh,
        in_specs=(
            P("fsdp", "tp"),
            P("fsdp", "tp"),
            P("fsdp", None),
            P("fsdp", None),
            P("fsdp", None, "tp"),
            P("fsdp", None, "tp"),
            P("fsdp", "tp", None),
            P("fsdp", None, "tp"),
            P("fsdp", None, "tp"),
            P("fsdp", "tp", None),
        ),
        out_specs=(P("fsdp", None, "tp"), P("fsdp", None, "tp"), P("fsdp", "tp", None)),
        check_vma=False,
    )
```

```python
import jax
import jax.numpy as jnp
from jax import lax
from jax.experimental import pallas as pl
from jax.experimental.pallas import tpu as pltpu
from jax.sharding import PartitionSpec as P

MESH = pl.DeviceIdType.MESH
CAPACITY = 12
BLOCK = 4 * CAPACITY
VMEM_LIMIT = 60 * 1024 * 1024
SPACE = pl.BlockSpec(memory_space=pltpu.VMEM)
HBM = pl.BlockSpec(memory_space=pl.ANY)


def layer_kernel(
    mine_ref, cotan_ref, route_ref, weight_ref, gate_ref, up_ref, gdir_ref, udir_ref, down_ref, ddir_ref,
    flip_out, cot_out, curved_out,
    flip_ref, cot_ref, curved_ref, send_ref, pick_ref, feed_ref, early_ref, first_ref, second_ref, packed_ref, tok_ref,
    fwd_ref, bwd_ref, part_ref, core_in, chip_keep, chip_out, chip_in,
    z_send, z_recv, x_send, x_recv, y_send, y_recv, early_y_send, early_y_recv, early_x_send, early_x_recv,
    load_sem, core_send, core_recv, chip_send, chip_recv, back_send, back_recv, last_send, last_recv, out_sem,
):
    tokens, width = mine_ref.shape
    fine = width // 4
    rows, depth = tok_ref.shape
    chunks, _, wide = curved_ref.shape
    slim = wide // 3
    parts = packed_ref.shape[0] // 4
    units = parts * chunks
    parted, halved, quarter = rows // parts, rows // parts // 2, rows // parts // 4
    experts = 4 * parts
    me, high = lax.axis_index("fsdp"), lax.axis_index("tp")
    z, low, x, core = me // 16, (me // 8) % 2, (me // 2) % 4, me % 2
    y = high * 2 + low
    facing = y + core * (3 - 2 * y)

    def plane(to_z, to_y):
        return to_z * 16 + (to_y % 2) * 8 + x * 2 + core, to_y // 2

    def beside(to_x, to_core):
        return me - x * 2 - core + to_x * 2 + to_core, high

    barrier = pltpu.get_barrier_semaphore()
    for step in range(1, 4):
        for there in (plane((z + step) % 4, facing), plane(z, (y + step) % 4)):
            pl.semaphore_signal(barrier, inc=1, device_id=there, device_id_type=MESH)
    for step in range(1, 8):
        pl.semaphore_signal(
            barrier, inc=1, device_id=beside((x + step // 2) % 4, (core + step) % 2), device_id_type=MESH
        )

    def loads(chunk):
        at = slice(chunk * slim, (chunk + 1) * slim)
        pieces = [
            (ref.at[:, at], fwd_ref.at[chunk, :, pl.ds(place * slim, slim)])
            for place, ref in enumerate((gate_ref, up_ref, gdir_ref, udir_ref))
        ] + [
            (ref.at[at, :], bwd_ref.at[chunk, pl.ds(place * slim, slim), :])
            for place, ref in enumerate((down_ref, ddir_ref))
        ]
        return [
            pltpu.make_async_copy(source, target, load_sem.at[chunk, place])
            for place, (source, target) in enumerate(pieces)
        ]

    row = route_ref[...].astype(jnp.float32)
    col = jnp.broadcast_to(row, (tokens, tokens)).T
    first = lax.broadcasted_iota(jnp.int32, (tokens, tokens), 0)
    second = lax.broadcasted_iota(jnp.int32, (tokens, tokens), 1)
    before = jnp.where((col == row) & (first < second), 1.0, 0.0)
    slot = row * CAPACITY + jnp.sum(before, axis=0, keepdims=True)
    key = jnp.concatenate([slot + 1024.0 * part for part in range(4)], axis=1)
    place = lax.broadcasted_iota(jnp.int32, (experts * BLOCK, 1), 0).astype(jnp.float32)
    number = jnp.floor((place + 0.5) * (1.0 / BLOCK))
    within = place - number * BLOCK
    span = jnp.floor((number + 0.5) * 0.25)
    pair = jnp.floor((number - 4.0 * span + 0.5) * 0.5)
    expert = 2.0 * number - 4.0 * span - 3.0 * pair
    part = jnp.floor((within + 0.5) * (1.0 / CAPACITY))
    wanted = expert * CAPACITY + (within - part * CAPACITY) + 1024.0 * part
    pick_ref[...] = jnp.where(wanted == key, 1.0, 0.0).astype(jnp.bfloat16)
    gate = jnp.broadcast_to(weight_ref[...], (tokens, tokens)).T[:, 0:1]
    weighted = (gate * cotan_ref[...].astype(jnp.float32)).astype(jnp.bfloat16)
    for piece in range(2):
        for side in range(2):
            lanes = slice((2 * piece + side) * fine, (2 * piece + side + 1) * fine)
            feed_ref[piece, pl.ds(side * tokens, tokens), :] = mine_ref[:, lanes]
            feed_ref[piece, pl.ds((2 + side) * tokens, tokens), :] = weighted[:, lanes]

    def gather(step, carry):
        at = pl.ds(pl.multiple_of(step * 4 * BLOCK, 4 * BLOCK), 4 * BLOCK)
        for piece in range(2):
            picked = jnp.dot(pick_ref[at, :], feed_ref[piece], preferred_element_type=jnp.float32)
            for place in range(4):
                send_ref[piece, step, place // 2, place % 2] = picked[
                    place * BLOCK : (place + 1) * BLOCK
                ].astype(jnp.bfloat16)
        return carry

    lax.fori_loop(0, parts, gather, 0)
    pl.semaphore_wait(barrier, 13)

    def transfer(here, source, target, send_sem, recv_sem, device):
        def start():
            @pl.when(here)
            def _():
                pltpu.make_async_copy(source, target, recv_sem).start()

            @pl.when(jnp.logical_not(here))
            def _():
                remote().start()

        def remote():
            return pltpu.make_async_remote_copy(
                src_ref=source, dst_ref=target, send_sem=send_sem, recv_sem=recv_sem,
                device_id=device, device_id_type=MESH,
            )

        def finish():
            @pl.when(jnp.logical_not(here))
            def _():
                remote().wait_send()

        return start, finish

    def landed(place, sem):
        pltpu.make_async_copy(place, place, sem).wait()

    def along_z(part, to_core):
        dz = part + part // 2 * (1 - 2 * (part % 2))
        to_z = (z + dz) % 4
        return transfer(
            jnp.logical_and(dz == 0, core == 0), send_ref.at[to_core, to_z], first_ref.at[part, to_core],
            z_send.at[part * 2 + to_core], z_recv.at[part * 2 + to_core], plane(to_z, facing),
        )

    def along_x(part, pair, to_core):
        to_x = pair * 2 + (high + core) % 2
        return transfer(
            jnp.logical_and(to_x == x, to_core == core),
            first_ref.at[part, to_core, pair],
            second_ref.at[part, :, pl.ds(pl.multiple_of(x * BLOCK, BLOCK), BLOCK), :],
            x_send.at[part * 4 + pair * 2 + to_core], x_recv.at[part * 4 + x], beside(to_x, to_core),
        )

    def along_y(part, to_low, to_high):
        to_y = to_high * 2 + to_low
        origin_core = (high + x) % 2
        origin = (low + origin_core * (1 - 2 * low)) * 2 + origin_core
        return transfer(
            to_y == y, second_ref.at[part, to_low], packed_ref.at[part * 4 + origin],
            y_send.at[part * 4 + to_y], y_recv.at[part * 4 + origin], plane(z, to_y),
        )

    def early_y(to_low, to_high):
        to_y = to_high * 2 + to_low
        return transfer(
            to_y == y, send_ref.at[:, z, :, to_low], early_ref.at[y],
            early_y_send.at[to_y], early_y_recv.at[y], plane(z, to_y),
        )

    def early_x(turn, pair, to_core):
        from_y = (y + turn) % 4
        origin = (from_y % 2) * 2 + core
        to_x = pair * 2 + from_y // 2
        return transfer(
            jnp.logical_and(to_x == x, to_core == core),
            early_ref.at[from_y, to_core, pair],
            packed_ref.at[origin, pl.ds(pl.multiple_of(x * BLOCK, BLOCK), BLOCK), :],
            early_x_send.at[turn * 4 + pair * 2 + to_core], early_x_recv.at[origin * 4 + x], beside(to_x, to_core),
        )

    def hop_early():
        for to_low in range(2):
            for to_high in range(2):
                early_y(to_low, to_high)[0]()

    def pass_early():
        for turn in (0, 1, 3, 2):
            from_y = (y + turn) % 4
            landed(early_ref.at[from_y], early_y_recv.at[from_y])
            for pair in range(2):
                for to_core in range(2):
                    early_x(turn, pair, to_core)[0]()

    def arrive_early():
        for origin in range(4):
            for number in range(4):
                landed(
                    packed_ref.at[origin, pl.ds(number * BLOCK, BLOCK), :], early_x_recv.at[origin * 4 + number]
                )

    def hop_z(part, carry):
        for to_core in range(2):
            along_z(part, to_core)[0]()
        return carry

    def hop_x(part):
        for to_core in range(2):
            landed(first_ref.at[part, to_core], z_recv.at[part * 2 + to_core])
            for pair in range(2):
                along_x(part, pair, to_core)[0]()

    def hop_y(part):
        for number in range(4):
            landed(second_ref.at[part, :, pl.ds(number * BLOCK, BLOCK), :], x_recv.at[part * 4 + number])
        for to_low in range(2):
            for to_high in range(2):
                along_y(part, to_low, to_high)[0]()

    def arrive(part):
        for number in range(4):
            landed(packed_ref.at[part * 4 + number], y_recv.at[part * 4 + number])

    hop_early()
    hop_z(1, 0)
    hop_z(2, 0)
    for chunk in range(chunks):
        for copy in loads(chunk):
            copy.start()

    sort_rows = 4 * BLOCK
    left = lax.broadcasted_iota(jnp.int32, (sort_rows, 1), 0).astype(jnp.float32)
    part = jnp.floor((left + 0.5) * (1.0 / BLOCK))
    source = jnp.floor((left - part * BLOCK + 0.5) * (1.0 / CAPACITY))
    rest = left - part * BLOCK - source * CAPACITY
    wanted = source * BLOCK + part * CAPACITY + rest
    have = lax.broadcasted_iota(jnp.int32, (1, sort_rows), 1).astype(jnp.float32)
    sorter = jnp.where(wanted == have, 1.0, 0.0).astype(jnp.bfloat16)

    def sort(group, carry):
        taken = packed_ref[group]
        ordered = jnp.dot(sorter, taken, preferred_element_type=jnp.float32).astype(jnp.bfloat16)
        to = pl.ds(pl.multiple_of(group * BLOCK, BLOCK), BLOCK)
        tok_ref[to, 0:fine] = ordered[0:BLOCK]
        tok_ref[to, fine:depth] = ordered[BLOCK : 2 * BLOCK]
        cot_ref[to, 0:fine] = ordered[2 * BLOCK : 3 * BLOCK]
        cot_ref[to, fine:depth] = ordered[3 * BLOCK : 4 * BLOCK]
        return carry


    against = (((1,), (1,)), ((), ()))

    chip = x % 2
    core_mate, chip_mate = beside(x, 1 - core), beside(x + 1 - 2 * chip, core)

    def to_core(unit):
        theirs = pl.ds(pl.multiple_of((1 - core) * halved, halved), halved)
        return pltpu.make_async_remote_copy(
            src_ref=part_ref.at[unit % 4, theirs, :], dst_ref=core_in.at[unit],
            send_sem=core_send.at[unit], recv_sem=core_recv.at[unit],
            device_id=core_mate, device_id_type=MESH,
        )

    def to_chip(unit):
        return pltpu.make_async_remote_copy(
            src_ref=chip_out.at[unit], dst_ref=chip_in.at[unit],
            send_sem=chip_send.at[unit], recv_sem=chip_recv.at[unit],
            device_id=chip_mate, device_id_type=MESH,
        )

    def back(unit, where):
        begin = unit // chunks * parted + core * halved + where * quarter
        place = curved_ref.at[unit % chunks, pl.ds(pl.multiple_of(begin, quarter), quarter), :]
        return pltpu.make_async_remote_copy(
            src_ref=place, dst_ref=place,
            send_sem=back_send.at[unit], recv_sem=back_recv.at[unit],
            device_id=chip_mate, device_id_type=MESH,
        )

    def last(unit, where):
        begin = unit // chunks * parted + where * halved
        place = curved_ref.at[unit % chunks, pl.ds(pl.multiple_of(begin, halved), halved), :]
        return pltpu.make_async_remote_copy(
            src_ref=place, dst_ref=place,
            send_sem=last_send.at[unit], recv_sem=last_recv.at[unit],
            device_id=core_mate, device_id_type=MESH,
        )

    def products(unit):
        @pl.when(unit < chunks)
        def _():
            for place in range(6):
                loaded = (
                    bwd_ref.at[unit, pl.ds(0, slim), :] if place >= 4 else fwd_ref.at[unit, :, pl.ds(0, slim)]
                )
                pltpu.make_async_copy(loaded, loaded, load_sem.at[unit, place]).wait()

        @pl.when(unit >= 4)
        def _():
            to_core(unit - 4).wait_send()

        chunk = unit % chunks
        at = pl.ds(pl.multiple_of(unit // chunks * parted, parted), parted)
        part_ref[unit % 4, :, 0 : 4 * slim] = jnp.dot(
            tok_ref[at, :], fwd_ref[chunk], preferred_element_type=jnp.float32
        )
        part_ref[unit % 4, :, 4 * slim : 6 * slim] = lax.dot_general(
            cot_ref[at, :], bwd_ref[chunk], against, preferred_element_type=jnp.float32
        )
        to_core(unit).start()

    def core_sum(unit):
        to_core(unit).wait_recv()
        slot = unit % 4

        def whole(where):
            own = pl.ds(pl.multiple_of(core * halved + where * quarter, quarter), quarter)
            return part_ref[slot, own, :] + core_in[unit, pl.ds(pl.multiple_of(where * quarter, quarter), quarter), :]

        chip_out[unit] = whole(1 - chip).astype(jnp.bfloat16)
        to_chip(unit).start()
        chip_keep[unit] = whole(chip)

    def partial_products(part):
        lax.fori_loop(part * 4, part * 4 + 4, sort, 0)

        def both(step, carry):
            @pl.when(step < chunks)
            def _():
                products(part * chunks + step)

            @pl.when(step > 0)
            def _():
                core_sum(part * chunks + step - 1)

            return carry

        lax.fori_loop(0, chunks + 1, both, 0)

    def curve(unit, carry):
        to_chip(unit).wait_recv()
        total = chip_keep[unit] + chip_in[unit].astype(jnp.float32)
        begin = unit // chunks * parted + core * halved + chip * quarter
        curved_ref[unit % chunks, pl.ds(pl.multiple_of(begin, quarter), quarter), :] = curvature(total, slim)
        back(unit, chip).start()
        return carry

    pass_early()
    hop_z(3, 0)
    hop_x(1)
    hop_x(2)
    hop_x(3)

    rows_out = [
        pltpu.make_async_copy(flip_ref, flip_out, out_sem.at[units]),
        pltpu.make_async_copy(cot_ref, cot_out, out_sem.at[units + 1]),
    ]

    def curved_copy(unit):
        at = pl.ds(pl.multiple_of(unit // chunks * parted, parted), parted)
        chunk = unit % chunks
        return pltpu.make_async_copy(curved_ref.at[chunk, at, :], curved_out.at[chunk, at, :], out_sem.at[unit])

    def advance(step, carry):
        @pl.when(step == 0)
        def _():
            arrive_early()
            hop_y(1)

        @pl.when(jnp.logical_and(step >= 1, step < parts))
        def _():
            arrive(step)

        @pl.when(jnp.logical_and(step >= 1, step + 1 < parts))
        def _():
            hop_y(step + 1)

        @pl.when(step == parts)
        def _():
            flip_ref[...] = tok_ref[...].T
            for copy in rows_out:
                copy.start()

        @pl.when(step < parts)
        def _():
            partial_products(step)

        @pl.when(step >= 1)
        def _():
            lax.fori_loop((step - 1) * chunks, (step - 1) * chunks + chunks, curve, 0)

        return carry

    lax.fori_loop(0, parts + 1, advance, 0)
    def spread(unit, carry):
        back(unit, 1 - chip).wait_recv()
        last(unit, core).start()
        return carry

    lax.fori_loop(0, units, spread, 0)

    def finish(unit, carry):
        last(unit, 1 - core).wait_recv()
        back(unit, chip).wait_send()
        last(unit, core).wait_send()
        curved_copy(unit).start()

        @pl.when(unit >= units - 4)
        def _():
            to_core(unit).wait_send()

        to_chip(unit).wait_send()
        return carry

    lax.fori_loop(0, units, finish, 0)
    def sent(part, carry):
        for first in range(2):
            along_z(part, first)[1]()
            for second in range(2):
                along_x(part, first, second)[1]()
                along_y(part, first, second)[1]()
        return carry

    lax.fori_loop(1, parts, sent, 0)
    for first in range(2):
        for second in range(2):
            early_y(first, second)[1]()
            for turn in range(4):
                early_x(turn, first, second)[1]()

    def written(unit, carry):
        curved_copy(unit).wait()
        return carry

    lax.fori_loop(0, units, written, 0)
    for copy in rows_out:
        copy.wait()


def curvature(total, width):
    gate_pre, up_pre, gate_tan, up_tan, grad_hidden, tan_grad = (
        total[:, width * place : width * (place + 1)] for place in range(6)
    )
    sigmoid_gate = jax.nn.sigmoid(gate_pre)
    silu_gate = gate_pre * sigmoid_gate
    slope = sigmoid_gate * (1.0 + gate_pre * (1.0 - sigmoid_gate))
    bend = sigmoid_gate * (1.0 - sigmoid_gate) * (2.0 + gate_pre * (1.0 - 2.0 * sigmoid_gate))
    tan_gate = (
        tan_grad * up_pre * slope
        + grad_hidden * up_tan * slope
        + grad_hidden * up_pre * bend * gate_tan
    )
    tan_up = tan_grad * silu_gate + grad_hidden * slope * gate_tan
    tan_hidden = slope * gate_tan * up_pre + silu_gate * up_tan
    return jnp.concatenate([tan_gate, tan_up, tan_hidden], axis=1).astype(jnp.bfloat16)


def product_kernel(
    flip_in, cot_in, curved_in, gate_out, up_out, down_out,
    flip_ref, cot_ref, curved_ref, gate_ref, up_ref, down_ref, load_sem, store_sem,
):
    chunks, _, wide = curved_ref.shape
    slim = wide // 3
    half = flip_ref.shape[0] // 2
    sides = [pl.ds(0, half), pl.ds(half, half)]
    curved_in_copy = [
        pltpu.make_async_copy(curved_in.at[chunk], curved_ref.at[chunk], load_sem.at[chunk])
        for chunk in range(chunks)
    ]
    flip_copy = [
        pltpu.make_async_copy(flip_in.at[side], flip_ref.at[side], load_sem.at[chunks + place])
        for place, side in enumerate(sides)
    ]
    cot_copy = pltpu.make_async_copy(cot_in, cot_ref, load_sem.at[chunks + 2])
    for copy in [curved_in_copy[0], *flip_copy, *curved_in_copy[1:], cot_copy]:
        copy.start()
    stores = []

    def store(source, target):
        copy = pltpu.make_async_copy(source, target, store_sem.at[len(stores)])
        copy.start()
        stores.append(copy)

    for chunk in range(chunks):
        curved_in_copy[chunk].wait()
        lanes = pl.ds(chunk * slim, slim)
        for place, side in enumerate(sides):
            if chunk == 0:
                flip_copy[place].wait()
            both = jnp.dot(
                flip_ref[side, :], curved_ref[chunk, :, 0 : 2 * slim], preferred_element_type=jnp.float32
            )
            gate_ref[side, lanes] = both[:, 0:slim]
            up_ref[side, lanes] = both[:, slim : 2 * slim]
            store(gate_ref.at[side, lanes], gate_out.at[side, lanes])
            store(up_ref.at[side, lanes], up_out.at[side, lanes])
    cot_copy.wait()
    for chunk in range(chunks):
        lanes = pl.ds(chunk * slim, slim)
        down_ref[lanes, :] = lax.dot_general(
            curved_ref[chunk, :, 2 * slim : 3 * slim],
            cot_ref[...],
            (((0,), (0,)), ((), ())),
            preferred_element_type=jnp.float32,
        )
        store(down_ref.at[lanes, :], down_out.at[lanes, :])
    for copy in stores:
        copy.wait()


def local(
    tokens, cotangent, routes, gates, gate_proj, up_proj, down_proj, gate_dir, up_dir, down_dir
):
    count, width = tokens.shape
    groups = lax.axis_size("fsdp")
    experts = groups // 4
    depth, hidden = gate_proj.shape[1:]
    rows = groups * CAPACITY
    slim = 256
    chunks = hidden // slim
    bf16, f32 = jnp.bfloat16, jnp.float32

    parts = 4
    units = parts * chunks
    parted = rows // parts
    flipped, cot, curved = pl.pallas_call(
        layer_kernel,
        name="layer",
        out_shape=(
            jax.ShapeDtypeStruct((depth, rows), bf16),
            jax.ShapeDtypeStruct((rows, depth), bf16),
            jax.ShapeDtypeStruct((chunks, rows, 3 * slim), bf16),
        ),
        in_specs=[SPACE] * 4 + [HBM] * 6,
        out_specs=(HBM,) * 3,
        scratch_shapes=[
            pltpu.VMEM((depth, rows), bf16),
            pltpu.VMEM((rows, depth), bf16),
            pltpu.VMEM((chunks, rows, 3 * slim), bf16),
            pltpu.VMEM((2, 4, 2, 2, BLOCK, width // 4), bf16),
            pltpu.VMEM((experts * BLOCK, 4 * count), bf16),
            pltpu.VMEM((2, 4 * count, width // 4), bf16),
            pltpu.VMEM((4, 2, 2, BLOCK, width // 4), bf16),
            pltpu.VMEM((parts, 2, 2, 2, BLOCK, width // 4), bf16),
            pltpu.VMEM((parts, 2, 4 * BLOCK, width // 4), bf16),
            pltpu.VMEM((parts * 4, 4 * BLOCK, width // 4), bf16),
            pltpu.VMEM((rows, depth), bf16),
            pltpu.VMEM((chunks, depth, 4 * slim), bf16),
            pltpu.VMEM((chunks, 2 * slim, depth), bf16),
            pltpu.VMEM((4, parted, 6 * slim), f32),
            pltpu.VMEM((units, parted // 2, 6 * slim), f32),
            pltpu.VMEM((units, parted // 4, 6 * slim), f32),
            pltpu.VMEM((units, parted // 4, 6 * slim), bf16),
            pltpu.VMEM((units, parted // 4, 6 * slim), bf16),
        ]
        + [pltpu.SemaphoreType.DMA((parts * 2,))] * 2
        + [pltpu.SemaphoreType.DMA((parts * 4,))] * 4
        + [pltpu.SemaphoreType.DMA((4,))] * 2
        + [pltpu.SemaphoreType.DMA((16,))] * 2
        + [pltpu.SemaphoreType.DMA((chunks, 6))]
        + [pltpu.SemaphoreType.DMA((units,))] * 8
        + [pltpu.SemaphoreType.DMA((units + 2,))],
        compiler_params=pltpu.CompilerParams(
            collective_id=0, has_side_effects=True, vmem_limit_bytes=VMEM_LIMIT
        ),
    )(
        tokens, cotangent, routes.reshape(1, count), gates.reshape(1, count),
        gate_proj[0], up_proj[0], gate_dir[0], up_dir[0], down_proj[0], down_dir[0],
    )

    hess_gate, hess_up, hess_down = pl.pallas_call(
        product_kernel,
        name="products",
        out_shape=(
            jax.ShapeDtypeStruct((depth, hidden), f32),
            jax.ShapeDtypeStruct((depth, hidden), f32),
            jax.ShapeDtypeStruct((hidden, depth), f32),
        ),
        in_specs=[HBM] * 3,
        out_specs=(HBM,) * 3,
        scratch_shapes=[
            pltpu.VMEM((depth, rows), bf16),
            pltpu.VMEM((rows, depth), bf16),
            pltpu.VMEM((chunks, rows, 3 * slim), bf16),
            pltpu.VMEM((depth, hidden), f32),
            pltpu.VMEM((depth, hidden), f32),
            pltpu.VMEM((hidden, depth), f32),
            pltpu.SemaphoreType.DMA((chunks + 3,)),
            pltpu.SemaphoreType.DMA((5 * chunks,)),
        ],
        compiler_params=pltpu.CompilerParams(vmem_limit_bytes=VMEM_LIMIT),
    )(flipped, cot, curved)
    return (hess_gate[None], hess_up[None], hess_down[None])


def solution(mesh):
    return jax.shard_map(
        local,
        mesh=mesh,
        in_specs=(
            P("fsdp", "tp"),
            P("fsdp", "tp"),
            P("fsdp", None),
            P("fsdp", None),
            P("fsdp", None, "tp"),
            P("fsdp", None, "tp"),
            P("fsdp", "tp", None),
            P("fsdp", None, "tp"),
            P("fsdp", None, "tp"),
            P("fsdp", "tp", None),
        ),
        out_specs=(P("fsdp", None, "tp"), P("fsdp", None, "tp"), P("fsdp", "tp", None)),
        check_vma=False,
    )
```
